256 devices in a mesh: rows: 32 (over y, x, core), cols: 8 (over z).
Axes of the slice: x: 4, y: 4, z: 8, core: 2. Of those that a mesh axis runs over, the one named last changes fastest.
Arguments:
- latent: float32 [2048, 16384], P('rows', 'cols'), may hold values from -3 to 3
- counts: int32 [2048, 16384], P('rows', 'cols'), may hold values from 0 to 39
- exposure: int32 [2048, 16384], P('rows', 'cols'), may hold values from 1 to 32
Outputs:
- newton_step: float32 [2048, 16384], P('rows', 'cols')
- residual: float32 [2048, 16384], P('rows', 'cols')
- direction: float32 [2048, 16384], P('rows', 'cols')
The draws below stay inside these ranges and needn't reach their ends.
All inputs are finite; a program needn't handle non-finite values.
Results may differ from the reference program's by a relative error of at most 0.0003.
Values sent between devices are 32-bit elements; how exact they have to be, the bound alone decides.
No kernel may reach another device: no remote copies, remote signals or barrier semaphores. Data moves between devices by JAX's collectives and lax.ppermute only.
A program may use at most 128 MiB of HBM per device.

```python
import jax
import jax.numpy as jnp
from jax import lax

ROWS_DEV = 64
NROWS = 2048
NCOLS = 16384


def draw_latent(key, part):
    row_line = jnp.arange(NROWS, dtype=jnp.float32)[:, None]
    ramp = row_line / NROWS
    noise = jax.random.normal(key, (NROWS, NCOLS), jnp.float32)
    return jnp.clip((0.25 + 0.75 * ramp) * noise, -3.0, 3.0)


def plant(result, key, low, top_value):
    longest = result.shape.index(max(result.shape))
    spots = []
    for shift in (0, 1):
        where = [jax.random.randint(jax.random.fold_in(key, axis), (), 0, length) for axis, length in enumerate(result.shape)]
        where[longest] = (where[longest] + shift) % result.shape[longest]
        spots.append(tuple(where))
    return result.at[spots[0]].set(low).at[spots[1]].set(top_value)


def setup_inputs(seed: int = 0) -> dict:
    arg_keys = jax.random.split(jax.random.key(seed), 4)
    latent = draw_latent(jax.random.fold_in(arg_keys[3], 71), 0)
    counts = plant(jax.random.randint(arg_keys[1], (NROWS, NCOLS), 0, 40), jax.random.fold_in(arg_keys[1], 1), 0, 39).astype(jnp.int32)
    exposure = plant(jax.random.randint(arg_keys[2], (NROWS, NCOLS), 1, 33), jax.random.fold_in(arg_keys[2], 1), 1, 32).astype(jnp.int32)
    return dict(latent=latent, counts=counts, exposure=exposure)


dispersion = 4.0
prior_scale = 0.25
kappa_sq = 0.05
weight_shift = 1.0


def prior_apply(grid_field):
    padded = jnp.pad(grid_field, 2)
    row_count, col_count = grid_field.shape

    def offset_view(shift_row, shift_col):
        return padded[2 + shift_row:2 + shift_row + row_count, 2 + shift_col:2 + shift_col + col_count]

    centre = kappa_sq + 4.0
    nearest = offset_view(1, 0) + offset_view(-1, 0) + offset_view(0, 1) + offset_view(0, -1)
    diagonal = offset_view(1, 1) + offset_view(1, -1) + offset_view(-1, 1) + offset_view(-1, -1)
    distant = offset_view(2, 0) + offset_view(-2, 0) + offset_view(0, 2) + offset_view(0, -2)
    return prior_scale * ((centre * centre + 4.0) * grid_field - 2.0 * centre * nearest + 2.0 * diagonal + distant)


def precondition(grid_field):
    bands = grid_field.reshape(NROWS // ROWS_DEV, ROWS_DEV, NCOLS)
    row_freq = jnp.arange(ROWS_DEV, dtype=jnp.float32)
    col_freq = jnp.arange(NCOLS, dtype=jnp.float32)
    col_whole = jnp.arange(NCOLS, dtype=jnp.int32)
    retained = (col_whole < NCOLS // 4) | (col_whole > NCOLS - NCOLS // 4)
    row_sine = jnp.sin(jnp.pi * row_freq / ROWS_DEV)
    col_sine = jnp.sin(jnp.pi * col_freq / NCOLS)
    inner_term = kappa_sq + 4.0 * row_sine[:, None] ** 2 + 4.0 * col_sine[None, :] ** 2
    symbol = prior_scale * inner_term * inner_term + weight_shift
    gain_table = jnp.where(retained[None, :], 1.0 / symbol, 1.0)

    def one_band(band_field):
        spectrum = jnp.fft.fft2(band_field) * gain_table
        return jnp.real(jnp.fft.ifft2(spectrum)).astype(jnp.float32)

    return lax.map(one_band, bands).reshape(NROWS, NCOLS)


def reference(latent, counts, exposure):
    mean_rate = exposure.astype(jnp.float32) * jnp.exp(latent)
    fisher = dispersion * mean_rate / (dispersion + mean_rate)
    score = (counts.astype(jnp.float32) - mean_rate) * dispersion / (dispersion + mean_rate)
    gradient = score - prior_apply(latent)
    first_search = precondition(gradient)
    first_product = jnp.sum(gradient * first_search)
    image = prior_apply(first_search) + fisher * first_search
    curvature = jnp.sum(first_search * image)
    step_size = first_product / curvature
    newton_step = step_size * first_search
    residual = gradient - step_size * image
    next_search = precondition(residual)
    next_product = jnp.sum(residual * next_search)
    direction = next_search + (next_product / first_product) * first_search
    return newton_step, residual, direction
```

```python
import functools
import math

import jax
import jax.numpy as jnp
import ml_dtypes
import numpy as np
from jax import lax
from jax.experimental import pallas as pl
from jax.experimental.pallas import tpu as pltpu
from jax.sharding import PartitionSpec as P

dispersion = 4.0
prior_scale = 0.25
kappa_sq = 0.05
weight_shift = 1.0
centre = kappa_sq + 4.0

band = 64
width = 2048
lanes = 128
tiles = width // lanes
parts = 8
total_cols = width * parts
lines = band // parts
half = 72
kept = 64
vmem_bytes = 48 * 1024 * 1024


def high_low(table):
    high = table.astype(ml_dtypes.bfloat16)
    low = (table - high.astype(np.float64)).astype(ml_dtypes.bfloat16)
    return high, low


@functools.cache
def tables():
    rows = np.arange(band)
    freq = np.zeros(band)
    basis = np.zeros((band, band))
    basis[0] = 1.0 / math.sqrt(band)
    for k in range(1, band // 2):
        angle = 2.0 * np.pi * ((k * rows) % band) / band
        basis[2 * k - 1] = np.cos(angle) * math.sqrt(2.0 / band)
        basis[2 * k] = np.sin(angle) * math.sqrt(2.0 / band)
        freq[2 * k - 1] = freq[2 * k] = k
    basis[band - 1] = (1.0 - 2.0 * (rows % 2)) / math.sqrt(band)
    freq[band - 1] = band // 2
    row_term = kappa_sq + 4.0 * np.sin(np.pi * freq / band) ** 2
    out = {}
    high, low = high_low(basis)
    out["row_forward"] = np.concatenate([high, high, low], 1)
    high, low = high_low(basis.T)
    out["row_inverse"] = np.concatenate([high, high, low], 1)
    out["row_term"] = np.tile(row_term[:, None], (1, lanes)).astype(np.float32)

    count = lanes // 2 + 1
    outer = np.arange(count)
    inner = np.arange(lanes)
    angle = 2.0 * np.pi * ((outer[:, None] * inner[None, :]) % lanes) / lanes
    section = np.zeros((2 * half, lanes))
    section[:count] = np.cos(angle)
    section[half : half + count] = np.sin(angle)
    high, low = high_low(section)
    out["outer_forward"] = np.concatenate([high, high, low], 1)
    section = section.T.copy()
    section[:, half:] *= -1.0
    high, low = high_low(section)
    out["outer_inverse"] = np.concatenate([high, high, low], 1)

    angle = 2.0 * np.pi * outer[:, None] * inner[None, :] / total_cols
    twist = np.zeros((2, half, lanes), np.float32)
    twist[0, :count] = np.cos(angle)
    twist[1, :count] = np.sin(angle)
    out["twist"] = twist

    kept_inner = np.concatenate([np.arange(kept // 2), np.arange(lanes - kept // 2, lanes)])
    angle = 2.0 * np.pi * ((inner[:, None] * kept_inner[None, :]) % lanes) / lanes
    cosine, sine = np.cos(angle), np.sin(angle)
    high, low = high_low(np.block([[cosine, -sine], [sine, cosine]]))
    out["inner_forward"] = np.concatenate([high, low], 1)
    high, low = high_low(np.block([[cosine.T, sine.T], [-sine.T, cosine.T]]))
    out["inner_inverse"] = np.concatenate([high, high, low], 0)

    col_freq = outer[:, None] + lanes * kept_inner[None, :]
    quarter = total_cols // 4
    retained = (col_freq < quarter) | (col_freq > total_cols - quarter)
    twice = np.where((outer == 0) | (outer == lanes // 2), 1.0, 2.0)[:, None]
    weight = np.zeros((half, 2 * kept))
    weight[:count] = np.tile(np.where(retained, twice / total_cols, 0.0), (1, 2))
    term = np.zeros((half, 2 * kept))
    term[:count] = np.tile(4.0 * np.sin(np.pi * col_freq / total_cols) ** 2, (1, 2))
    out["weight"] = weight.astype(np.float32)
    out["col_term"] = term.astype(np.float32)
    return out


def split(value):
    high = value.astype(jnp.bfloat16)
    low = (value - high.astype(jnp.float32)).astype(jnp.bfloat16)
    return high, low


def dot(left, right):
    return jnp.dot(left, right, preferred_element_type=jnp.float32)


def left_product(table, value):
    high, low = split(value)
    return dot(table, jnp.concatenate([high, low, high], 0))


def lane_index(shape):
    return lax.broadcasted_iota(jnp.int32, shape, 1)


def stencil(pad):
    full = width + lanes
    field = pad[8:72, :]
    near = pad[7:71, :] + pad[9:73, :]
    far = pad[6:70, :] + pad[10:74, :]
    beside = 2.0 * near - (2.0 * centre) * field
    across = pltpu.roll(beside, 1, 1) + pltpu.roll(beside, full - 1, 1)
    distant = far + pltpu.roll(field, 2, 1) + pltpu.roll(field, full - 2, 1)
    return prior_scale * ((centre * centre + 4.0) * field - 2.0 * centre * near + across + distant)


def store_coefs(coefs, out, count):
    for part in range(parts):
        for tile in range(count):
            out[part, tile * lines : (tile + 1) * lines, :] = coefs[
                part * lines : (part + 1) * lines, tile * lanes : (tile + 1) * lanes
            ]


def load_coefs(ref, count):
    return jnp.concatenate(
        [
            jnp.concatenate(
                [ref[part, tile * lines : (tile + 1) * lines, :] for part in range(parts)], 0
            )
            for tile in range(count)
        ],
        1,
    )


def gradient_kernel(
    place, latent, counts, exposure, swap_a, swap_b, basis, payload, grad, beyond, fisher, pad
):
    even = place[0] % 2 == 0
    pad[8:72, :width] = latent[...]
    pad[6:8, :width] = jnp.where(even, swap_b[...], swap_a[...])
    pad[72:74, :width] = jnp.where(even, swap_a[...], swap_b[...])
    pad[0:80, width:] = jnp.zeros((80, lanes), jnp.float32)
    prior = stencil(pad)
    mean_rate = exposure[...].astype(jnp.float32) * jnp.exp(latent[...])
    ratio = dispersion / (dispersion + mean_rate)
    fisher[...] = mean_rate * ratio
    score = (counts[...].astype(jnp.float32) - mean_rate) * ratio
    inside = score - prior[:, :width]
    outside = -prior[:, width:]
    grad[...] = inside
    beyond[...] = outside
    coefs = left_product(basis[...], jnp.concatenate([inside, outside], 1))
    store_coefs(coefs, payload, tiles + 1)


def filter_kernel(
    place,
    incoming,
    row_term,
    col_term,
    weight,
    outer_forward,
    outer_inverse,
    inner_forward,
    inner_inverse,
    twist,
    out,
    energy,
    *,
    edges,
):
    lane = lane_index((tiles, lanes))
    sub = lax.broadcasted_iota(jnp.int32, (tiles, lanes), 0)
    first = (sub == 0) & (lane < lanes // 2)
    last = (sub == tiles - 1) & (lane >= lanes // 2)
    line_fields = []
    for line in range(lines):
        blocks = [
            incoming[part, pl.ds(line, tiles, stride=lines), :] for part in range(parts)
        ]
        if edges:
            spill = [
                incoming[part, tiles * lines + line : tiles * lines + line + 1, :]
                for part in range(parts)
            ]
            for part in range(parts):
                if part > 0:
                    blocks[part] = blocks[part] + jnp.where(first, spill[part - 1], 0.0)
                if part < parts - 1:
                    blocks[part] = blocks[part] + jnp.where(last, spill[part + 1], 0.0)
        line_fields.append(jnp.concatenate(blocks, 0))
    field = jnp.concatenate(line_fields, 1)
    section = left_product(outer_forward[...], field)
    cosine, sine = twist[0], twist[1]
    turned = []
    for line in range(lines):
        cols = slice(line * lanes, (line + 1) * lanes)
        even_part, odd_part = section[:half, cols], section[half:, cols]
        real = even_part * cosine - odd_part * sine
        imag = -(odd_part * cosine + even_part * sine)
        turned.append(jnp.concatenate([real, imag], 1))
    high, low = split(jnp.concatenate(turned, 0))
    both = dot(high, inner_forward[...])
    spectrum = both[:, : 2 * kept] + both[:, 2 * kept :] + dot(low, inner_forward[:, : 2 * kept])
    row_line = row_term[pl.ds(pl.multiple_of(place[1] * lines, lines), lines), :]
    scaled = []
    total = jnp.zeros((half, 2 * kept), jnp.float32)
    for line in range(lines):
        inner_term = row_line[line : line + 1, :] + col_term[...]
        quad = prior_scale * inner_term * inner_term
        gain = -quad / (quad + weight_shift) * weight[...]
        piece = spectrum[line * half : (line + 1) * half, :]
        scaled.append(piece * gain)
        if not edges:
            total = total + piece * scaled[-1]
    if not edges:
        energy[...] = jnp.broadcast_to(jnp.sum(total, axis=(0, 1), keepdims=True), (8, lanes))
    high, low = split(jnp.concatenate(scaled, 0))
    back = dot(jnp.concatenate([high, low], 1), inner_inverse[: 4 * kept, :]) + dot(
        high, inner_inverse[4 * kept :, :]
    )
    reals, imags = [], []
    for line in range(lines):
        rows = slice(line * half, (line + 1) * half)
        real, imag = back[rows, :lanes], back[rows, lanes:]
        reals.append(real * cosine - imag * sine)
        imags.append(imag * cosine + real * sine)
    folded = jnp.concatenate([jnp.concatenate(reals, 1), jnp.concatenate(imags, 1)], 0)
    result = left_product(outer_inverse[...], folded)
    edge_lane = lane_index((1, lanes)) < lanes // 2
    for line in range(lines):
        cols = slice(line * lanes, (line + 1) * lanes)
        for part in range(parts):
            out[part, pl.ds(line, tiles, stride=lines), :] = result[
                part * tiles : (part + 1) * tiles, cols
            ]
        if edges:
            for part in range(parts):
                nothing = jnp.zeros((1, lanes), jnp.float32)
                after, before = nothing, nothing
                if part < parts - 1:
                    row = slice((part + 1) * tiles, (part + 1) * tiles + 1)
                    after = result[row, cols] + field[row, cols]
                if part > 0:
                    row = slice(part * tiles - 1, part * tiles)
                    before = result[row, cols] + field[row, cols]
                out[part, tiles * lines + line : tiles * lines + line + 1, :] = jnp.where(
                    edge_lane, after, before
                )


def search_kernel(place, incoming, grad, left, right, basis, full_grad, search, send_a, send_b):
    even = place[0] % 2 == 0
    coefs = load_coefs(incoming, tiles + 1)
    update = left_product(basis[...], coefs)
    lane = lane_index((band, lanes))
    head = grad[:, :lanes] + jnp.where(lane < lanes // 2, left[...], 0.0)
    tail = grad[:, width - lanes :] + jnp.where(lane >= lanes // 2, right[...], 0.0)
    whole = jnp.concatenate([head, grad[:, lanes : width - lanes], tail], 1)
    full_grad[...] = whole
    found = jnp.concatenate([whole + update[:, :width], update[:, width:]], 1)
    search[...] = found
    top, bottom = found[:2, :], found[band - 2 :, :]
    send_a[...] = jnp.where(even, bottom, top)
    send_b[...] = jnp.where(even, top, bottom)


def image_kernel(
    place, search, swap_a, swap_b, fisher, grad, basis, payload, image, sums, pad
):
    even = place[0] % 2 == 0
    pad[8:72, :] = search[...]
    pad[6:8, :] = jnp.where(even, swap_b[...], swap_a[...])
    pad[72:74, :] = jnp.where(even, swap_a[...], swap_b[...])
    prior = stencil(pad)
    field = search[:, :width]
    result = prior[:, :width] + fisher[...] * field
    image[...] = result
    products = (grad[...] * field, field * result, result * result)
    for row, product in enumerate(products):
        total = jnp.sum(product, axis=(0, 1), keepdims=True)
        sums[row : row + 1, :] = jnp.broadcast_to(total, (1, lanes))
    sums[3:8, :] = jnp.zeros((5, lanes), jnp.float32)
    store_coefs(left_product(basis[...], result), payload, tiles)


def second_kernel(incoming, image, basis, second):
    second[...] = image[...] + left_product(basis[...], load_coefs(incoming, tiles))


def final_kernel(sums, search, grad, image, second, step, residual, direction):
    total = jnp.sum(sums[...], axis=0)
    first_product = total[0:1, 0:1]
    curvature = total[1:2, 0:1]
    image_product = total[2:3, 0:1]
    step_size = first_product / curvature
    ratio = step_size * (image_product / curvature) - 1.0
    field = search[:, :width]
    step[...] = step_size * field
    residual[...] = grad[...] - step_size * image[...]
    direction[...] = (field - step_size * second[...]) + ratio * field


def call(kernel, shapes, args, scratch=(), flops=0):
    in_specs = [pl.BlockSpec(memory_space=pltpu.SMEM if a.dtype == jnp.int32 and a.ndim == 1 else pltpu.VMEM) for a in args]
    outs = tuple(jax.ShapeDtypeStruct(s, jnp.float32) for s in shapes)
    moved = 4 * (sum(a.size for a in args) + sum(o.size for o in outs))
    return pl.pallas_call(
        kernel,
        out_shape=outs,
        in_specs=in_specs,
        out_specs=tuple(pl.BlockSpec(memory_space=pltpu.VMEM) for _ in outs),
        scratch_shapes=list(scratch),
        compiler_params=pltpu.CompilerParams(vmem_limit_bytes=vmem_bytes),
        cost_estimate=pl.CostEstimate(flops=flops, bytes_accessed=moved, transcendentals=0),
    )(*args)


def row_swaps():
    count = lax.axis_size("rows")
    inner = [(i, i ^ 1) for i in range(count)]
    outer = [(i, i + 1) for i in range(1, count - 1, 2)] + [(i + 1, i) for i in range(1, count - 1, 2)]
    return inner, outer


def swap_rows(send_a, send_b):
    inner, outer = row_swaps()
    return lax.ppermute(send_a, "rows", inner), lax.ppermute(send_b, "rows", outer)


def exchange(payload):
    return lax.all_to_all(payload, "cols", split_axis=0, concat_axis=0, tiled=True)


def sum_over_rows(value):
    count = lax.axis_size("rows")

    def swap(mask):
        return lax.ppermute(value, "rows", [(i, i ^ mask) for i in range(count)])

    value = value + swap(1)
    value = value + swap(2) + swap(4) + swap(6)
    return value + swap(8) + swap(16) + swap(24)


def on_device(latent, counts, exposure):
    consts = tables()
    tab = {name: jnp.asarray(value) for name, value in consts.items()}
    row_index = lax.axis_index("rows")
    place = jnp.stack([row_index, lax.axis_index("cols")]).astype(jnp.int32)
    pad = pltpu.VMEM((80, width + lanes), jnp.float32)
    wide = (parts, (tiles + 1) * lines, lanes)
    slim = (parts, tiles * lines, lanes)
    block = (band, width)
    filters = [
        tab[name]
        for name in (
            "row_term",
            "col_term",
            "weight",
            "outer_forward",
            "outer_inverse",
            "inner_forward",
            "inner_inverse",
            "twist",
        )
    ]

    even = row_index % 2 == 0
    top, bottom = latent[:2], latent[band - 2 :]
    swap_a, swap_b = swap_rows(jnp.where(even, bottom, top), jnp.where(even, top, bottom))
    payload, grad_part, beyond, fisher = call(
        gradient_kernel,
        (wide, block, (band, lanes), block),
        (place, latent, counts, exposure, swap_a, swap_b, tab["row_forward"]),
        (pad,),
        flops=10**8,
    )
    incoming = exchange(payload)
    ends = parts - 1
    from_left = lax.ppermute(beyond, "cols", [(i, i + 1) for i in range(ends)])
    from_right = lax.ppermute(beyond, "cols", [(i + 1, i) for i in range(ends)])
    back, _ = call(
        functools.partial(filter_kernel, edges=True),
        (wide, (8, lanes)),
        (place, incoming, *filters),
        flops=10**9,
    )
    incoming = exchange(back)
    grad, search, send_a, send_b = call(
        search_kernel,
        (block, (band, width + lanes), (2, width + lanes), (2, width + lanes)),
        (place, incoming, grad_part, from_left, from_right, tab["row_inverse"]),
        flops=10**8,
    )
    swap_a, swap_b = swap_rows(send_a, send_b)
    payload, image, sums = call(
        image_kernel,
        (slim, block, (8, lanes)),
        (place, search, swap_a, swap_b, fisher, grad, tab["row_forward"]),
        (pad,),
        flops=10**8,
    )
    incoming = exchange(payload)
    back, energy = call(
        functools.partial(filter_kernel, edges=False),
        (slim, (8, lanes)),
        (place, incoming, *filters),
        flops=10**9,
    )
    incoming = exchange(back)
    image_row = lax.broadcasted_iota(jnp.int32, (8, lanes), 0) == 2
    sums = sum_over_rows(sums + jnp.where(image_row, energy, 0.0))
    sums = exchange(jnp.broadcast_to(sums[None], (parts, 8, lanes)))
    (second,) = call(second_kernel, (block,), (incoming, image, tab["row_inverse"]), flops=10**8)
    return call(
        final_kernel, (block, block, block), (sums, search, grad, image, second), flops=10**6
    )


def solution(mesh):
    placed = (P("rows", "cols"), P("rows", "cols"), P("rows", "cols"))
    return jax.shard_map(
        on_device,
        mesh=mesh,
        in_specs=placed,
        out_specs=placed,
        check_vma=False,
    )
```

```python
import functools
import math

import jax
import jax.numpy as jnp
import ml_dtypes
import numpy as np
from jax import lax
from jax.experimental import pallas as pl
from jax.experimental.pallas import tpu as pltpu
from jax.sharding import PartitionSpec as P

dispersion = 4.0
prior_scale = 0.25
kappa_sq = 0.05
weight_shift = 1.0
centre = kappa_sq + 4.0

band = 64
width = 2048
lanes = 128
tiles = width // lanes
parts = 8
total_cols = width * parts
lines = band // parts
half = 72
kept = 64
vmem_bytes = 48 * 1024 * 1024


def high_low(table):
    high = table.astype(ml_dtypes.bfloat16)
    low = (table - high.astype(np.float64)).astype(ml_dtypes.bfloat16)
    return high, low


@functools.cache
def tables():
    rows = np.arange(band)
    freq = np.zeros(band)
    basis = np.zeros((band, band))
    basis[0] = 1.0 / math.sqrt(band)
    for k in range(1, band // 2):
        angle = 2.0 * np.pi * ((k * rows) % band) / band
        basis[2 * k - 1] = np.cos(angle) * math.sqrt(2.0 / band)
        basis[2 * k] = np.sin(angle) * math.sqrt(2.0 / band)
        freq[2 * k - 1] = freq[2 * k] = k
    basis[band - 1] = (1.0 - 2.0 * (rows % 2)) / math.sqrt(band)
    freq[band - 1] = band // 2
    row_term = kappa_sq + 4.0 * np.sin(np.pi * freq / band) ** 2
    out = {}
    high, low = high_low(basis)
    out["row_forward"] = np.concatenate([high, high, low], 1)
    share = np.zeros((band, 16))
    for row, at in ((0, 0), (1, 1), (2, band - 2), (3, band - 1)):
        share[:, row] = prior_scale * basis[:, at]
    share[:, 8 + 1] = prior_scale * basis[:, 0]
    share[:, 8 + 2] = prior_scale * basis[:, band - 1]
    high, low = high_low(share)
    out["halo_forward"] = np.concatenate([high, high, low], 1)
    high, low = high_low(basis.T)
    out["row_inverse"] = np.concatenate([high, high, low], 1)
    out["row_term"] = np.tile(row_term[:, None], (1, lanes)).astype(np.float32)

    count = lanes // 2 + 1
    outer = np.arange(count)
    inner = np.arange(lanes)
    angle = 2.0 * np.pi * ((outer[:, None] * inner[None, :]) % lanes) / lanes
    section = np.zeros((2 * half, lanes))
    section[:count] = np.cos(angle)
    section[half : half + count] = np.sin(angle)
    high, low = high_low(section)
    out["outer_forward"] = np.concatenate([high, high, low], 1)
    section = section.T.copy()
    section[:, half:] *= -1.0
    high, low = high_low(section)
    out["outer_inverse"] = np.concatenate([high, high, low], 1)

    angle = 2.0 * np.pi * outer[:, None] * inner[None, :] / total_cols
    twist = np.zeros((2, half, lanes), np.float32)
    twist[0, :count] = np.cos(angle)
    twist[1, :count] = np.sin(angle)
    out["twist"] = twist

    kept_inner = np.concatenate([np.arange(kept // 2), np.arange(lanes - kept // 2, lanes)])
    angle = 2.0 * np.pi * ((inner[:, None] * kept_inner[None, :]) % lanes) / lanes
    cosine, sine = np.cos(angle), np.sin(angle)
    high, low = high_low(np.block([[cosine, -sine], [sine, cosine]]))
    out["inner_forward"] = np.concatenate([high, low], 1)
    high, low = high_low(np.block([[cosine.T, sine.T], [-sine.T, cosine.T]]))
    out["inner_inverse"] = np.concatenate([high, high, low], 0)

    col_freq = outer[:, None] + lanes * kept_inner[None, :]
    quarter = total_cols // 4
    retained = (col_freq < quarter) | (col_freq > total_cols - quarter)
    twice = np.where((outer == 0) | (outer == lanes // 2), 1.0, 2.0)[:, None]
    weight = np.zeros((half, 2 * kept))
    weight[:count] = np.tile(np.where(retained, twice / total_cols, 0.0), (1, 2))
    term = np.zeros((half, 2 * kept))
    term[:count] = np.tile(4.0 * np.sin(np.pi * col_freq / total_cols) ** 2, (1, 2))
    out["weight"] = weight.astype(np.float32)
    out["col_term"] = term.astype(np.float32)
    return out


def split(value):
    high = value.astype(jnp.bfloat16)
    low = (value - high.astype(jnp.float32)).astype(jnp.bfloat16)
    return high, low


def dot(left, right):
    return jnp.dot(left, right, preferred_element_type=jnp.float32)


def left_product(table, value):
    high, low = split(value)
    return dot(table, jnp.concatenate([high, low, high], 0))


def lane_index(shape):
    return lax.broadcasted_iota(jnp.int32, shape, 1)


def neighbours(field):
    full = field.shape[1]
    return pltpu.roll(field, 1, 1) + pltpu.roll(field, full - 1, 1)


def stencil(pad):
    full = width + lanes
    field = pad[8:72, :]
    near = pad[7:71, :] + pad[9:73, :]
    far = pad[6:70, :] + pad[10:74, :]
    across = neighbours(2.0 * near - (2.0 * centre) * field)
    distant = far + pltpu.roll(field, 2, 1) + pltpu.roll(field, full - 2, 1)
    return prior_scale * ((centre * centre + 4.0) * field - 2.0 * centre * near + across + distant)


def halo_terms(place, swap_a, swap_b, halo):
    even = place[0] % 2 == 0
    span = swap_a.shape[1]
    halo[...] = jnp.zeros((8, width + lanes), jnp.float32)
    halo[0:2, :span] = jnp.where(even, swap_b[...], swap_a[...])
    halo[2:4, :span] = jnp.where(even, swap_a[...], swap_b[...])
    rows = halo[...]
    beside = 2.0 * neighbours(rows) - (2.0 * centre) * rows
    return rows, beside


def halo_rows(rows, beside):
    return prior_scale * jnp.concatenate(
        [
            beside[1:2] + rows[0:1],
            rows[1:2],
            jnp.zeros((4, width + lanes), jnp.float32),
            rows[2:3],
            beside[2:3] + rows[3:4],
        ],
        0,
    )


def add_halo_rows(field, added):
    index = lax.broadcasted_iota(jnp.int32, added.shape, 0)
    return jnp.concatenate(
        [
            field[:8] + jnp.where(index < 4, added, 0.0),
            field[8 : band - 8],
            field[band - 8 :] + jnp.where(index >= 4, added, 0.0),
        ],
        0,
    )


def store_coefs(place, coefs, buffer, outs, count):
    for part in range(parts):
        for tile in range(count):
            buffer[part, tile * lines : (tile + 1) * lines, :] = coefs[
                part * lines : (part + 1) * lines, tile * lanes : (tile + 1) * lanes
            ]
    store_blocks(place, buffer, outs)


def store_blocks(place, buffer, outs):
    for mask, out in enumerate(outs):
        out[...] = buffer[place[1] ^ mask]


def load_blocks(place, refs, buffer):
    for mask, ref in enumerate(refs):
        buffer[place[1] ^ mask] = ref[...]


def load_coefs(buffer, count):
    return jnp.concatenate(
        [
            jnp.concatenate(
                [buffer[part, tile * lines : (tile + 1) * lines, :] for part in range(parts)], 0
            )
            for tile in range(count)
        ],
        1,
    )


def gradient_kernel(latent, counts, exposure, basis, coefs, grad, fisher, pad):
    pad[0:8, :] = jnp.zeros((8, width + lanes), jnp.float32)
    pad[72:80, :] = jnp.zeros((8, width + lanes), jnp.float32)
    pad[8:72, :width] = latent[...]
    pad[8:72, width:] = jnp.zeros((band, lanes), jnp.float32)
    prior = stencil(pad)
    mean_rate = exposure[...].astype(jnp.float32) * jnp.exp(latent[...])
    ratio = dispersion / (dispersion + mean_rate)
    fisher[...] = mean_rate * ratio
    score = (counts[...].astype(jnp.float32) - mean_rate) * ratio
    inside = score - prior[:, :width]
    grad[...] = inside
    coefs[...] = left_product(basis[...], jnp.concatenate([inside, -prior[:, width:]], 1))


def gradient_halo_kernel(place, coefs, swap_a, swap_b, basis, *rest):
    outs, (added, halo, buffer) = rest[:parts], rest[parts:]
    rows, beside = halo_terms(place, swap_a, swap_b, halo)
    added[...] = -halo_rows(rows, beside)
    whole = coefs[...] - left_product(basis[...], jnp.concatenate([rows, beside], 0))
    spill = whole[:, width:]
    spill = spill + pltpu.roll(spill, lanes // 2, 1)
    store_coefs(place, jnp.concatenate([whole[:, :width], spill], 1), buffer, outs, tiles + 1)


def filter_kernel(place, *rest, edges):
    blocks_in, rest = rest[:parts], rest[parts:]
    (
        sums,
        row_term,
        col_term,
        weight,
        outer_forward,
        outer_inverse,
        inner_forward,
        inner_inverse,
        twist,
    ) = rest[:9]
    blocks_out, (incoming, out) = rest[9 : 9 + parts], rest[9 + parts :]
    load_blocks(place, blocks_in, incoming)
    lane = lane_index((tiles, lanes))
    sub = lax.broadcasted_iota(jnp.int32, (tiles, lanes), 0)
    first = (sub == 0) & (lane < 2)
    last = (sub == tiles - 1) & (lane >= lanes - 2)
    line_fields = []
    for line in range(lines):
        blocks = [
            incoming[part, pl.ds(line, tiles, stride=lines), :] for part in range(parts)
        ]
        if edges:
            spill = [
                incoming[part, tiles * lines + line : tiles * lines + line + 1, :]
                for part in range(parts)
            ]
            for part in range(parts):
                if part > 0:
                    blocks[part] = blocks[part] + jnp.where(first, spill[part - 1], 0.0)
                if part < parts - 1:
                    blocks[part] = blocks[part] + jnp.where(last, spill[part + 1], 0.0)
        line_fields.append(jnp.concatenate(blocks, 0))
    field = jnp.concatenate(line_fields, 1)
    section = left_product(outer_forward[...], field)
    cosine, sine = twist[0], twist[1]
    turned = []
    for line in range(lines):
        cols = slice(line * lanes, (line + 1) * lanes)
        even_part, odd_part = section[:half, cols], section[half:, cols]
        real = even_part * cosine - odd_part * sine
        imag = -(odd_part * cosine + even_part * sine)
        turned.append(jnp.concatenate([real, imag], 1))
    high, low = split(jnp.concatenate(turned, 0))
    both = dot(high, inner_forward[...])
    spectrum = both[:, : 2 * kept] + both[:, 2 * kept :] + dot(low, inner_forward[:, : 2 * kept])
    row_line = row_term[pl.ds(pl.multiple_of(place[1] * lines, lines), lines), :]
    scaled = []
    total = jnp.zeros((half, 2 * kept), jnp.float32)
    for line in range(lines):
        inner_term = row_line[line : line + 1, :] + col_term[...]
        quad = prior_scale * inner_term * inner_term
        gain = -quad / (quad + weight_shift) * weight[...]
        piece = spectrum[line * half : (line + 1) * half, :]
        scaled.append(piece * gain)
        if not edges:
            total = total + piece * scaled[-1]
    if not edges:
        energy = jnp.sum(total, axis=(0, 1), keepdims=True)
        third = lax.broadcasted_iota(jnp.int32, (8, lanes), 0) == 2
        known = sums[...] + jnp.where(third, energy, 0.0)
        for part in range(parts):
            out[part, tiles * lines :, :] = known
    high, low = split(jnp.concatenate(scaled, 0))
    back = dot(jnp.concatenate([high, low], 1), inner_inverse[: 4 * kept, :]) + dot(
        high, inner_inverse[4 * kept :, :]
    )
    reals, imags = [], []
    for line in range(lines):
        rows = slice(line * half, (line + 1) * half)
        real, imag = back[rows, :lanes], back[rows, lanes:]
        reals.append(real * cosine - imag * sine)
        imags.append(imag * cosine + real * sine)
    folded = jnp.concatenate([jnp.concatenate(reals, 1), jnp.concatenate(imags, 1)], 0)
    result = left_product(outer_inverse[...], folded)
    edge_lane = lane_index((1, lanes))
    nothing = jnp.zeros((1, lanes), jnp.float32)
    for line in range(lines):
        cols = slice(line * lanes, (line + 1) * lanes)
        for part in range(parts):
            out[part, pl.ds(line, tiles, stride=lines), :] = result[
                part * tiles : (part + 1) * tiles, cols
            ]
        if edges:
            spot = tiles * lines + line
            for part in range(parts):
                after, before, from_left, from_right = nothing, nothing, nothing, nothing
                if part < parts - 1:
                    row = slice((part + 1) * tiles, (part + 1) * tiles + 1)
                    after = result[row, cols] + field[row, cols]
                    from_right = incoming[part + 1, spot : spot + 1, :]
                if part > 0:
                    row = slice(part * tiles - 1, part * tiles)
                    before = result[row, cols] + field[row, cols]
                    from_left = incoming[part - 1, spot : spot + 1, :]
                middle = jnp.where(edge_lane >= lanes // 2, from_left, from_right)
                out[part, spot : spot + 1, :] = jnp.where(
                    edge_lane < 2, after, jnp.where(edge_lane >= lanes - 2, before, middle)
                )
    store_blocks(place, out, blocks_out)


def search_kernel(place, *rest):
    blocks, (grad, added, basis, full_grad, search, send_a, send_b, buffer) = (
        rest[:parts],
        rest[parts:],
    )
    even = place[0] % 2 == 0
    load_blocks(place, blocks, buffer)
    update = left_product(basis[...], load_coefs(buffer, tiles + 1))
    beyond = update[:, width:]
    spill = pltpu.roll(beyond, lanes // 2, 1)
    lane = lane_index((band, lanes))
    base = add_halo_rows(grad[...], added[:, :width])
    head = base[:, :lanes] + jnp.where(lane < 2, spill, 0.0)
    tail = base[:, width - lanes :] + jnp.where(lane >= lanes - 2, spill, 0.0)
    whole = jnp.concatenate([head, base[:, lanes : width - lanes], tail], 1)
    full_grad[...] = whole
    found = jnp.concatenate([whole + update[:, :width], beyond], 1)
    search[...] = found
    top, bottom = found[:2, :], found[band - 2 :, :]
    send_a[...] = jnp.where(even, bottom, top)
    send_b[...] = jnp.where(even, top, bottom)


def image_kernel(search, fisher, basis, coefs, image, pad):
    pad[0:8, :] = jnp.zeros((8, width + lanes), jnp.float32)
    pad[72:80, :] = jnp.zeros((8, width + lanes), jnp.float32)
    pad[8:72, :] = search[...]
    result = stencil(pad)[:, :width] + fisher[...] * search[:, :width]
    image[...] = result
    coefs[...] = left_product(basis[...], result)


def image_halo_kernel(place, coefs, swap_a, swap_b, basis, *rest):
    outs, (added, halo, buffer) = rest[:parts], rest[parts:]
    rows, beside = halo_terms(place, swap_a, swap_b, halo)
    added[...] = halo_rows(rows, beside)
    both = jnp.concatenate([rows, beside], 0)[:, :width]
    store_coefs(place, coefs[...] + left_product(basis[...], both), buffer, outs, tiles)


def sums_kernel(search, grad, partial, added, image, sums):
    field = search[:, :width]
    result = add_halo_rows(partial[...], added[:, :width])
    image[...] = result
    products = (grad[...] * field, field * result, result * result)
    for row, product in enumerate(products):
        total = jnp.sum(product, axis=(0, 1), keepdims=True)
        sums[row : row + 1, :] = jnp.broadcast_to(total, (1, lanes))
    sums[3:8, :] = jnp.zeros((5, lanes), jnp.float32)


def second_kernel(place, *rest):
    blocks, (image, basis, second, spread, buffer) = rest[:parts], rest[parts:]
    load_blocks(place, blocks, buffer)
    total = buffer[0, tiles * lines :, :]
    for part in range(1, parts):
        total = total + buffer[part, tiles * lines :, :]
    for row in range(spread.shape[0]):
        spread[row] = total
    second[...] = image[...] + left_product(basis[...], load_coefs(buffer, tiles))


def final_kernel(sums, search, grad, image, second, step, residual, direction):
    total = jnp.sum(sums[...], axis=0)
    first_product = total[0:1, 0:1]
    curvature = total[1:2, 0:1]
    image_product = total[2:3, 0:1]
    step_size = first_product / curvature
    ratio = step_size * (image_product / curvature) - 1.0
    field = search[:, :width]
    step[...] = step_size * field
    residual[...] = grad[...] - step_size * image[...]
    direction[...] = (field - step_size * second[...]) + ratio * field


def call(kernel, shapes, args, scratch=(), flops=0):
    in_specs = [pl.BlockSpec(memory_space=pltpu.SMEM if a.dtype == jnp.int32 and a.ndim == 1 else pltpu.VMEM) for a in args]
    outs = tuple(jax.ShapeDtypeStruct(s, jnp.float32) for s in shapes)
    moved = 4 * (sum(a.size for a in args) + sum(o.size for o in outs))
    return pl.pallas_call(
        kernel,
        out_shape=outs,
        in_specs=in_specs,
        out_specs=tuple(pl.BlockSpec(memory_space=pltpu.VMEM) for _ in outs),
        scratch_shapes=list(scratch),
        compiler_params=pltpu.CompilerParams(vmem_limit_bytes=vmem_bytes),
        cost_estimate=pl.CostEstimate(flops=flops, bytes_accessed=moved, transcendentals=0),
    )(*args)


def row_swaps():
    count = lax.axis_size("rows")
    inner = [(i, i ^ 1) for i in range(count)]
    outer = [(i, i + 1) for i in range(1, count - 1, 2)] + [(i + 1, i) for i in range(1, count - 1, 2)]
    return inner, outer


def exchange(blocks):
    count = lax.axis_size("cols")
    got = {}
    for mask in (4, 3, 5, 2, 6, 1, 7):
        got[mask] = lax.ppermute(blocks[mask], "cols", [(i, i ^ mask) for i in range(count)])
    return [blocks[0]] + [got[mask] for mask in range(1, parts)]


def swap_rows(send_a, send_b):
    inner, outer = row_swaps()
    return lax.ppermute(send_a, "rows", inner), lax.ppermute(send_b, "rows", outer)


def on_device(latent, counts, exposure):
    consts = tables()
    tab = {name: jnp.asarray(value) for name, value in consts.items()}
    row_index = lax.axis_index("rows")
    place = jnp.stack([row_index, lax.axis_index("cols")]).astype(jnp.int32)
    full = width + lanes
    pad = pltpu.VMEM((80, full), jnp.float32)
    halo = pltpu.VMEM((8, full), jnp.float32)
    wide = ((tiles + 1) * lines, lanes)
    slim = (tiles * lines, lanes)
    wide_buffer = pltpu.VMEM((parts, *wide), jnp.float32)
    slim_buffer = pltpu.VMEM((parts, *slim), jnp.float32)
    block = (band, width)
    extended = (band, full)
    filters = [
        tab[name]
        for name in (
            "row_term",
            "col_term",
            "weight",
            "outer_forward",
            "outer_inverse",
            "inner_forward",
            "inner_inverse",
            "twist",
        )
    ]

    even = row_index % 2 == 0
    top, bottom = latent[:2], latent[band - 2 :]
    swap_a, swap_b = swap_rows(jnp.where(even, bottom, top), jnp.where(even, top, bottom))
    coefs, grad_part, fisher = call(
        gradient_kernel,
        (extended, block, block),
        (latent, counts, exposure, tab["row_forward"]),
        (pad,),
        flops=10**9,
    )
    *blocks, added = call(
        gradient_halo_kernel,
        (wide,) * parts + ((8, full),),
        (place, coefs, swap_a, swap_b, tab["halo_forward"]),
        (halo, wide_buffer),
        flops=10**7,
    )
    blocks = exchange(blocks)
    blocks = call(
        functools.partial(filter_kernel, edges=True),
        (wide,) * parts,
        (place, *blocks, jnp.zeros((8, lanes), jnp.float32), *filters),
        (wide_buffer, wide_buffer),
        flops=10**9,
    )
    blocks = exchange(blocks)
    grad, search, send_a, send_b = call(
        search_kernel,
        (block, extended, (2, full), (2, full)),
        (place, *blocks, grad_part, added, tab["row_inverse"]),
        (wide_buffer,),
        flops=10**8,
    )
    swap_a, swap_b = swap_rows(send_a, send_b)
    coefs, partial = call(
        image_kernel,
        (block, block),
        (search, fisher, tab["row_forward"]),
        (pad,),
        flops=10**9,
    )
    *blocks, added = call(
        image_halo_kernel,
        (slim,) * parts + ((8, full),),
        (place, coefs, swap_a, swap_b, tab["halo_forward"]),
        (halo, slim_buffer),
        flops=10**7,
    )
    blocks = exchange(blocks)
    image, sums = call(
        sums_kernel, (block, (8, lanes)), (search, grad, partial, added), flops=10**8
    )
    blocks = call(
        functools.partial(filter_kernel, edges=False),
        (wide,) * parts,
        (place, *blocks, sums, *filters),
        (slim_buffer, wide_buffer),
        flops=10**9,
    )
    blocks = exchange(blocks)
    second, spread = call(
        second_kernel,
        (block, (lax.axis_size("rows"), 8, lanes)),
        (place, *blocks, image, tab["row_inverse"]),
        (wide_buffer,),
        flops=10**8,
    )
    sums = lax.all_to_all(spread, "rows", split_axis=0, concat_axis=0, tiled=True)
    return call(
        final_kernel, (block, block, block), (sums, search, grad, image, second), flops=10**6
    )


def solution(mesh):
    placed = (P("rows", "cols"), P("rows", "cols"), P("rows", "cols"))
    return jax.shard_map(
        on_device,
        mesh=mesh,
        in_specs=placed,
        out_specs=placed,
        check_vma=False,
    )
```

```python
import functools
import math

import jax
import jax.numpy as jnp
import ml_dtypes
import numpy as np
from jax import lax
from jax.experimental import pallas as pl
from jax.experimental.pallas import tpu as pltpu
from jax.sharding import PartitionSpec as P

dispersion = 4.0
prior_scale = 0.25
kappa_sq = 0.05
weight_shift = 1.0
centre = kappa_sq + 4.0

band = 64
width = 2048
lanes = 128
tiles = width // lanes
parts = 8
total_cols = width * parts
lines = band // parts
half = 72
kept = 64
vmem_bytes = 48 * 1024 * 1024
pieces = 4
pairwise = (True, True, True, False)


def high_low(table):
    high = table.astype(ml_dtypes.bfloat16)
    low = (table - high.astype(np.float64)).astype(ml_dtypes.bfloat16)
    return high, low


@functools.cache
def tables():
    rows = np.arange(band)
    freq = np.zeros(band)
    basis = np.zeros((band, band))
    basis[0] = 1.0 / math.sqrt(band)
    for k in range(1, band // 2):
        angle = 2.0 * np.pi * ((k * rows) % band) / band
        basis[2 * k - 1] = np.cos(angle) * math.sqrt(2.0 / band)
        basis[2 * k] = np.sin(angle) * math.sqrt(2.0 / band)
        freq[2 * k - 1] = freq[2 * k] = k
    basis[band - 1] = (1.0 - 2.0 * (rows % 2)) / math.sqrt(band)
    freq[band - 1] = band // 2
    row_term = kappa_sq + 4.0 * np.sin(np.pi * freq / band) ** 2
    out = {}
    high, low = high_low(basis)
    out["row_forward"] = np.concatenate([high, high, low], 1)
    share = np.zeros((band, 16))
    for row, at in ((0, 0), (1, 1), (2, band - 2), (3, band - 1)):
        share[:, row] = prior_scale * basis[:, at]
    share[:, 8 + 1] = prior_scale * basis[:, 0]
    share[:, 8 + 2] = prior_scale * basis[:, band - 1]
    high, low = high_low(share)
    out["halo_forward"] = np.concatenate([high, high, low], 1)
    high, low = high_low(basis.T)
    out["row_inverse"] = np.concatenate([high, high, low], 1)
    out["row_term"] = np.tile(row_term[:, None], (1, lanes)).astype(np.float32)

    count = lanes // 2 + 1
    outer = np.arange(count)
    inner = np.arange(lanes)
    angle = 2.0 * np.pi * ((outer[:, None] * inner[None, :]) % lanes) / lanes
    section = np.zeros((2 * half, lanes))
    section[:count] = np.cos(angle)
    section[half : half + count] = np.sin(angle)
    high, low = high_low(section)
    out["outer_forward"] = np.concatenate([high, high, low], 1)
    section = section.T.copy()
    section[:, half:] *= -1.0
    high, low = high_low(section)
    out["outer_inverse"] = np.concatenate([high, high, low], 1)

    angle = 2.0 * np.pi * outer[:, None] * inner[None, :] / total_cols
    twist = np.zeros((2, half, lanes), np.float32)
    twist[0, :count] = np.cos(angle)
    twist[1, :count] = np.sin(angle)
    out["twist"] = twist

    kept_inner = np.concatenate([np.arange(kept // 2), np.arange(lanes - kept // 2, lanes)])
    angle = 2.0 * np.pi * ((inner[:, None] * kept_inner[None, :]) % lanes) / lanes
    cosine, sine = np.cos(angle), np.sin(angle)
    high, low = high_low(np.block([[cosine, -sine], [sine, cosine]]))
    out["inner_forward"] = np.concatenate([high, low], 1)
    high, low = high_low(np.block([[cosine.T, sine.T], [-sine.T, cosine.T]]))
    out["inner_inverse"] = np.concatenate([high, high, low], 0)

    col_freq = outer[:, None] + lanes * kept_inner[None, :]
    quarter = total_cols // 4
    retained = (col_freq < quarter) | (col_freq > total_cols - quarter)
    twice = np.where((outer == 0) | (outer == lanes // 2), 1.0, 2.0)[:, None]
    weight = np.zeros((half, 2 * kept))
    weight[:count] = np.tile(np.where(retained, twice / total_cols, 0.0), (1, 2))
    term = np.zeros((half, 2 * kept))
    term[:count] = np.tile(4.0 * np.sin(np.pi * col_freq / total_cols) ** 2, (1, 2))
    out["weight"] = weight.astype(np.float32)
    out["col_term"] = term.astype(np.float32)
    return out


def split(value):
    high = value.astype(jnp.bfloat16)
    low = (value - high.astype(jnp.float32)).astype(jnp.bfloat16)
    return high, low


def dot(left, right):
    return jnp.dot(left, right, preferred_element_type=jnp.float32)


def left_product(table, value):
    high, low = split(value)
    return dot(table, jnp.concatenate([high, low, high], 0))


def lane_index(shape):
    return lax.broadcasted_iota(jnp.int32, shape, 1)


def neighbours(field):
    full = field.shape[1]
    return pltpu.roll(field, 1, 1) + pltpu.roll(field, full - 1, 1)


def stencil(pad):
    full = width + lanes
    field = pad[8:72, :]
    near = pad[7:71, :] + pad[9:73, :]
    far = pad[6:70, :] + pad[10:74, :]
    across = neighbours(2.0 * near - (2.0 * centre) * field)
    distant = far + pltpu.roll(field, 2, 1) + pltpu.roll(field, full - 2, 1)
    return prior_scale * ((centre * centre + 4.0) * field - 2.0 * centre * near + across + distant)


def halo_terms(place, swap_a, swap_b, halo):
    even = place[0] % 2 == 0
    span = swap_a.shape[1]
    halo[...] = jnp.zeros((8, width + lanes), jnp.float32)
    halo[0:2, :span] = jnp.where(even, swap_b[...], swap_a[...])
    halo[2:4, :span] = jnp.where(even, swap_a[...], swap_b[...])
    rows = halo[...]
    beside = 2.0 * neighbours(rows) - (2.0 * centre) * rows
    return rows, beside


def halo_rows(rows, beside):
    return prior_scale * jnp.concatenate(
        [
            beside[1:2] + rows[0:1],
            rows[1:2],
            jnp.zeros((4, width + lanes), jnp.float32),
            rows[2:3],
            beside[2:3] + rows[3:4],
        ],
        0,
    )


def add_halo_rows(field, added):
    index = lax.broadcasted_iota(jnp.int32, added.shape, 0)
    return jnp.concatenate(
        [
            field[:8] + jnp.where(index < 4, added, 0.0),
            field[8 : band - 8],
            field[band - 8 :] + jnp.where(index >= 4, added, 0.0),
        ],
        0,
    )


def store_coefs(place, coefs, buffer, outs, count):
    target = outs[0] if len(outs) == 1 else buffer
    for part in range(parts):
        for tile in range(count):
            target[part, tile * lines : (tile + 1) * lines, :] = coefs[
                part * lines : (part + 1) * lines, tile * lanes : (tile + 1) * lanes
            ]
    store_blocks(place, buffer, outs)


def store_blocks(place, buffer, outs):
    if len(outs) == 1:
        return
    for mask, out in enumerate(outs):
        out[...] = buffer[place[1] ^ mask]


def load_blocks(place, refs, buffer):
    if len(refs) == 1:
        return refs[0]
    for mask, ref in enumerate(refs):
        buffer[place[1] ^ mask] = ref[...]
    return buffer


def load_coefs(buffer, count):
    return jnp.concatenate(
        [
            jnp.concatenate(
                [buffer[part, tile * lines : (tile + 1) * lines, :] for part in range(parts)], 0
            )
            for tile in range(count)
        ],
        1,
    )


def gradient_kernel(
    latent, counts, exposure, basis, coefs, grad, fisher, pad, counts_here, exposure_here, sems
):
    fields = ((latent, pad), (exposure, exposure_here), (counts, counts_here))
    copies = []
    for which, (there, here) in enumerate(fields):
        skip = 8 if which == 0 else 0
        for part in range(pieces):
            rows = pl.ds(part * (band // pieces), band // pieces)
            onto = pl.ds(part * (band // pieces) + skip, band // pieces)
            copies.append(
                pltpu.make_async_copy(
                    there.at[rows, :], here.at[onto, :width], sems.at[which, part]
                )
            )
            copies[-1].start()
    pad[0:8, :] = jnp.zeros((8, width + lanes), jnp.float32)
    pad[72:80, :] = jnp.zeros((8, width + lanes), jnp.float32)
    pad[8:72, width:] = jnp.zeros((band, lanes), jnp.float32)
    for copy in copies[:pieces]:
        copy.wait()
    prior = stencil(pad)
    for copy in copies[pieces:]:
        copy.wait()
    mean_rate = exposure_here[...].astype(jnp.float32) * jnp.exp(pad[8:72, :width])
    ratio = dispersion / (dispersion + mean_rate)
    fisher[...] = mean_rate * ratio
    score = (counts_here[...].astype(jnp.float32) - mean_rate) * ratio
    inside = score - prior[:, :width]
    grad[...] = inside
    coefs[...] = left_product(basis[...], jnp.concatenate([inside, -prior[:, width:]], 1))


def gradient_halo_kernel(place, coefs, swap_a, swap_b, basis, *rest):
    *outs, added, halo, buffer = rest
    rows, beside = halo_terms(place, swap_a, swap_b, halo)
    added[...] = -halo_rows(rows, beside)
    whole = coefs[...] - left_product(basis[...], jnp.concatenate([rows, beside], 0))
    spill = whole[:, width:]
    spill = spill + pltpu.roll(spill, lanes // 2, 1)
    store_coefs(place, jnp.concatenate([whole[:, :width], spill], 1), buffer, outs, tiles + 1)


def filter_kernel(place, *rest, edges, taken, given):
    blocks_in, rest = rest[:taken], rest[taken:]
    (
        sums,
        row_term,
        col_term,
        weight,
        outer_forward,
        outer_inverse,
        inner_forward,
        inner_inverse,
        twist,
    ) = rest[:9]
    blocks_out, (known, incoming, out) = rest[9 : 9 + given], rest[9 + given :]
    incoming = load_blocks(place, blocks_in, incoming)
    if given == 1:
        out = blocks_out[0]
    lane = lane_index((tiles, lanes))
    sub = lax.broadcasted_iota(jnp.int32, (tiles, lanes), 0)
    first = (sub == 0) & (lane < 2)
    last = (sub == tiles - 1) & (lane >= lanes - 2)
    if edges:
        known[...] = sums[...]
    line_fields = []
    for line in range(lines):
        blocks = [
            incoming[part, pl.ds(line, tiles, stride=lines), :] for part in range(parts)
        ]
        if edges:
            spill = [
                incoming[part, tiles * lines + line : tiles * lines + line + 1, :]
                for part in range(parts)
            ]
            for part in range(parts):
                if part > 0:
                    blocks[part] = blocks[part] + jnp.where(first, spill[part - 1], 0.0)
                if part < parts - 1:
                    blocks[part] = blocks[part] + jnp.where(last, spill[part + 1], 0.0)
        line_fields.append(jnp.concatenate(blocks, 0))
    field = jnp.concatenate(line_fields, 1)
    section = left_product(outer_forward[...], field)
    cosine, sine = twist[0], twist[1]
    turned = []
    for line in range(lines):
        cols = slice(line * lanes, (line + 1) * lanes)
        even_part, odd_part = section[:half, cols], section[half:, cols]
        real = even_part * cosine - odd_part * sine
        imag = -(odd_part * cosine + even_part * sine)
        turned.append(jnp.concatenate([real, imag], 1))
    high, low = split(jnp.concatenate(turned, 0))
    both = dot(high, inner_forward[...])
    spectrum = both[:, : 2 * kept] + both[:, 2 * kept :] + dot(low, inner_forward[:, : 2 * kept])
    row_line = row_term[pl.ds(pl.multiple_of(place[1] * lines, lines), lines), :]
    scaled = []
    total = jnp.zeros((half, 2 * kept), jnp.float32)
    for line in range(lines):
        inner_term = row_line[line : line + 1, :] + col_term[...]
        quad = prior_scale * inner_term * inner_term
        gain = -quad / (quad + weight_shift) * weight[...]
        piece = spectrum[line * half : (line + 1) * half, :]
        scaled.append(piece * gain)
        if not edges:
            total = total + piece * scaled[-1]
    if not edges:
        energy = jnp.sum(total, axis=(0, 1), keepdims=True)
        known[...] = sums[...] + jnp.where(lane_index((1, lanes)) == 2, energy, 0.0)
    high, low = split(jnp.concatenate(scaled, 0))
    back = dot(jnp.concatenate([high, low], 1), inner_inverse[: 4 * kept, :]) + dot(
        high, inner_inverse[4 * kept :, :]
    )
    reals, imags = [], []
    for line in range(lines):
        rows = slice(line * half, (line + 1) * half)
        real, imag = back[rows, :lanes], back[rows, lanes:]
        reals.append(real * cosine - imag * sine)
        imags.append(imag * cosine + real * sine)
    folded = jnp.concatenate([jnp.concatenate(reals, 1), jnp.concatenate(imags, 1)], 0)
    result = left_product(outer_inverse[...], folded)
    edge_lane = lane_index((1, lanes))
    nothing = jnp.zeros((1, lanes), jnp.float32)
    for line in range(lines):
        cols = slice(line * lanes, (line + 1) * lanes)
        for part in range(parts):
            out[part, pl.ds(line, tiles, stride=lines), :] = result[
                part * tiles : (part + 1) * tiles, cols
            ]
        if edges:
            spot = tiles * lines + line
            for part in range(parts):
                after, before, from_left, from_right = nothing, nothing, nothing, nothing
                if part < parts - 1:
                    row = slice((part + 1) * tiles, (part + 1) * tiles + 1)
                    after = result[row, cols] + field[row, cols]
                    from_right = incoming[part + 1, spot : spot + 1, :]
                if part > 0:
                    row = slice(part * tiles - 1, part * tiles)
                    before = result[row, cols] + field[row, cols]
                    from_left = incoming[part - 1, spot : spot + 1, :]
                middle = jnp.where(edge_lane >= lanes // 2, from_left, from_right)
                out[part, spot : spot + 1, :] = jnp.where(
                    edge_lane < 2, after, jnp.where(edge_lane >= lanes - 2, before, middle)
                )
    store_blocks(place, out, blocks_out)


def search_kernel(place, *rest):
    *blocks, grad, added, basis, full_grad, search, send_a, send_b, buffer = rest
    even = place[0] % 2 == 0
    buffer = load_blocks(place, blocks, buffer)
    update = left_product(basis[...], load_coefs(buffer, tiles + 1))
    beyond = update[:, width:]
    spill = pltpu.roll(beyond, lanes // 2, 1)
    lane = lane_index((band, lanes))
    base = add_halo_rows(grad[...], added[:, :width])
    head = base[:, :lanes] + jnp.where(lane < 2, spill, 0.0)
    tail = base[:, width - lanes :] + jnp.where(lane >= lanes - 2, spill, 0.0)
    whole = jnp.concatenate([head, base[:, lanes : width - lanes], tail], 1)
    full_grad[...] = whole
    found = jnp.concatenate([whole + update[:, :width], beyond], 1)
    search[...] = found
    top, bottom = found[:2, :], found[band - 2 :, :]
    send_a[...] = jnp.where(even, bottom, top)
    send_b[...] = jnp.where(even, top, bottom)


def image_kernel(search, fisher, basis, coefs, image, pad):
    pad[0:8, :] = jnp.zeros((8, width + lanes), jnp.float32)
    pad[72:80, :] = jnp.zeros((8, width + lanes), jnp.float32)
    pad[8:72, :] = search[...]
    result = stencil(pad)[:, :width] + fisher[...] * search[:, :width]
    image[...] = result
    coefs[...] = left_product(basis[...], result)


def image_halo_kernel(place, coefs, swap_a, swap_b, basis, *rest):
    *outs, added, halo, buffer = rest
    rows, beside = halo_terms(place, swap_a, swap_b, halo)
    added[...] = halo_rows(rows, beside)
    both = jnp.concatenate([rows, beside], 0)[:, :width]
    store_coefs(place, coefs[...] + left_product(basis[...], both), buffer, outs, tiles)


def sums_kernel(search, grad, partial, added, image, sums):
    field = search[:, :width]
    result = add_halo_rows(partial[...], added[:, :width])
    image[...] = result
    products = (grad[...] * field, field * result, result * result)
    lane = lane_index((1, lanes))
    line = jnp.zeros((1, lanes), jnp.float32)
    for which, product in enumerate(products):
        total = jnp.sum(product, axis=(0, 1), keepdims=True)
        line = line + jnp.where(lane == which, total, 0.0)
    sums[...] = line


def spread_kernel(one, two, three, four, spread):
    total = (one[...] + two[...]) + (three[...] + four[...])
    for part in range(parts):
        spread[part] = total


def second_kernel(place, *rest):
    *blocks, image, basis, second, buffer = rest
    buffer = load_blocks(place, blocks, buffer)
    second[...] = image[...] + left_product(basis[...], load_coefs(buffer, tiles))


def final_kernel(
    sums, search, grad, image, second, step, residual, direction, step_here, residual_here, direction_here, sems
):
    total = jnp.sum(sums[...], axis=0)
    first_product = total[0:1, 0:1]
    curvature = total[0:1, 1:2]
    image_product = total[0:1, 2:3]
    step_size = first_product / curvature
    ratio = step_size * (image_product / curvature) - 1.0
    copies = []
    for part in range(pieces):
        rows = slice(part * (band // pieces), (part + 1) * (band // pieces))
        field = search[rows, :width]
        results = (
            (step_size * field, step_here, step),
            (grad[rows, :] - step_size * image[rows, :], residual_here, residual),
            ((field - step_size * second[rows, :]) + ratio * field, direction_here, direction),
        )
        for which, (value, here, there) in enumerate(results):
            here[rows, :] = value
            copies.append(
                pltpu.make_async_copy(here.at[rows, :], there.at[rows, :], sems.at[which, part])
            )
            copies[-1].start()
    for copy in copies:
        copy.wait()


def call(kernel, shapes, args, scratch=(), flops=0, far=0, far_out=False):
    in_specs = [
        pl.BlockSpec(memory_space=pltpu.HBM if i < far else pltpu.VMEM) for i in range(len(args))
    ]
    if args[0].ndim == 1:
        in_specs[0] = pl.BlockSpec(memory_space=pltpu.SMEM)
    outs = tuple(jax.ShapeDtypeStruct(s, jnp.float32) for s in shapes)
    moved = 4 * (sum(a.size for a in args) + sum(o.size for o in outs))
    return pl.pallas_call(
        kernel,
        out_shape=outs,
        in_specs=in_specs,
        out_specs=tuple(
            pl.BlockSpec(memory_space=pltpu.HBM if far_out else pltpu.VMEM) for _ in outs
        ),
        scratch_shapes=list(scratch),
        compiler_params=pltpu.CompilerParams(vmem_limit_bytes=vmem_bytes),
        cost_estimate=pl.CostEstimate(flops=flops, bytes_accessed=moved, transcendentals=0),
    )(*args)


def row_swaps():
    count = lax.axis_size("rows")
    inner = [(i, i ^ 1) for i in range(count)]
    outer = [(i, i + 1) for i in range(1, count - 1, 2)] + [(i + 1, i) for i in range(1, count - 1, 2)]
    return inner, outer


def exchange(blocks):
    if len(blocks) == 1:
        return [lax.all_to_all(blocks[0], "cols", split_axis=0, concat_axis=0, tiled=True)]
    count = lax.axis_size("cols")
    got = {}
    for mask in (4, 3, 5, 2, 6, 1, 7):
        got[mask] = lax.ppermute(blocks[mask], "cols", [(i, i ^ mask) for i in range(count)])
    return [blocks[0]] + [got[mask] for mask in range(1, parts)]


def swap_rows(send_a, send_b):
    inner, outer = row_swaps()
    return lax.ppermute(send_a, "rows", inner), lax.ppermute(send_b, "rows", outer)


def sum_over_rows(value):
    count = lax.axis_size("rows")

    def swap(mask):
        return lax.ppermute(value, "rows", [(i, i ^ mask) for i in range(count)])

    value = value + swap(1)
    value = value + swap(2) + swap(4) + swap(6)
    return value, swap(8), swap(16), swap(24)


def on_device(latent, counts, exposure):
    consts = tables()
    tab = {name: jnp.asarray(value) for name, value in consts.items()}
    row_index = lax.axis_index("rows")
    place = jnp.stack([row_index, lax.axis_index("cols")]).astype(jnp.int32)
    full = width + lanes
    pad = pltpu.VMEM((80, full), jnp.float32)
    halo = pltpu.VMEM((8, full), jnp.float32)
    wide = ((tiles + 1) * lines, lanes)
    slim = (tiles * lines, lanes)
    wide_buffer = pltpu.VMEM((parts, *wide), jnp.float32)
    slim_buffer = pltpu.VMEM((parts, *slim), jnp.float32)
    def sent(shape, pairwise):
        return (shape,) * parts if pairwise else ((parts, *shape),)

    block = (band, width)
    extended = (band, full)
    filters = [
        tab[name]
        for name in (
            "row_term",
            "col_term",
            "weight",
            "outer_forward",
            "outer_inverse",
            "inner_forward",
            "inner_inverse",
            "twist",
        )
    ]

    even = row_index % 2 == 0
    top, bottom = latent[:2], latent[band - 2 :]
    swap_a, swap_b = swap_rows(jnp.where(even, bottom, top), jnp.where(even, top, bottom))
    coefs, grad_part, fisher = call(
        gradient_kernel,
        (extended, block, block),
        (
            *(pltpu.with_memory_space_constraint(a, pltpu.HBM) for a in (latent, counts, exposure)),
            tab["row_forward"],
        ),
        (
            pad,
            pltpu.VMEM(block, jnp.int32),
            pltpu.VMEM(block, jnp.int32),
            pltpu.SemaphoreType.DMA((3, pieces)),
        ),
        flops=10**9,
        far=3,
    )
    *blocks, added = call(
        gradient_halo_kernel,
        sent(wide, pairwise[0]) + ((8, full),),
        (place, coefs, swap_a, swap_b, tab["halo_forward"]),
        (halo, wide_buffer),
        flops=10**7,
    )
    blocks = exchange(blocks)
    *blocks, _ = call(
        functools.partial(
            filter_kernel, edges=True, taken=len(blocks), given=parts if pairwise[1] else 1
        ),
        (*sent(wide, pairwise[1]), (1, lanes)),
        (place, *blocks, jnp.zeros((1, lanes), jnp.float32), *filters),
        (wide_buffer, wide_buffer),
        flops=10**9,
    )
    blocks = exchange(blocks)
    grad, search, send_a, send_b = call(
        search_kernel,
        (block, extended, (2, full), (2, full)),
        (place, *blocks, grad_part, added, tab["row_inverse"]),
        (wide_buffer,),
        flops=10**8,
    )
    swap_a, swap_b = swap_rows(send_a, send_b)
    coefs, partial = call(
        image_kernel,
        (block, block),
        (search, fisher, tab["row_forward"]),
        (pad,),
        flops=10**9,
    )
    *blocks, added = call(
        image_halo_kernel,
        sent(slim, pairwise[2]) + ((8, full),),
        (place, coefs, swap_a, swap_b, tab["halo_forward"]),
        (halo, slim_buffer),
        flops=10**7,
    )
    blocks = exchange(blocks)
    image, sums = call(
        sums_kernel, (block, (1, lanes)), (search, grad, partial, added), flops=10**8
    )
    *blocks, known = call(
        functools.partial(
            filter_kernel, edges=False, taken=len(blocks), given=parts if pairwise[3] else 1
        ),
        (*sent(slim, pairwise[3]), (1, lanes)),
        (place, *blocks, sums, *filters),
        (slim_buffer, slim_buffer),
        flops=10**9,
    )
    blocks = exchange(blocks)
    (spread,) = call(spread_kernel, ((parts, 1, lanes),), sum_over_rows(known))
    sums = exchange([spread])[0]
    (second,) = call(
        second_kernel,
        (block,),
        (place, *blocks, image, tab["row_inverse"]),
        (slim_buffer,),
        flops=10**8,
    )
    return call(
        final_kernel,
        (block, block, block),
        (sums, search, grad, image, second),
        (pltpu.VMEM(block, jnp.float32),) * 3 + (pltpu.SemaphoreType.DMA((3, pieces)),),
        flops=10**6,
        far_out=True,
    )


def solution(mesh):
    placed = (P("rows", "cols"), P("rows", "cols"), P("rows", "cols"))
    return jax.shard_map(
        on_device,
        mesh=mesh,
        in_specs=placed,
        out_specs=placed,
        check_vma=False,
    )
```

```python
import functools
import math

import jax
import jax.numpy as jnp
import ml_dtypes
import numpy as np
from jax import lax
from jax.experimental import pallas as pl
from jax.experimental.pallas import tpu as pltpu
from jax.sharding import PartitionSpec as P

dispersion = 4.0
prior_scale = 0.25
kappa_sq = 0.05
weight_shift = 1.0
centre = kappa_sq + 4.0

band = 64
width = 2048
lanes = 128
tiles = width // lanes
parts = 8
total_cols = width * parts
lines = band // parts
half = 72
kept = 64
vmem_bytes = 48 * 1024 * 1024
pieces = 4


def high_low(table):
    high = table.astype(ml_dtypes.bfloat16)
    low = (table - high.astype(np.float64)).astype(ml_dtypes.bfloat16)
    return high, low


@functools.cache
def tables():
    rows = np.arange(band)
    freq = np.zeros(band)
    basis = np.zeros((band, band))
    basis[0] = 1.0 / math.sqrt(band)
    for k in range(1, band // 2):
        angle = 2.0 * np.pi * ((k * rows) % band) / band
        basis[2 * k - 1] = np.cos(angle) * math.sqrt(2.0 / band)
        basis[2 * k] = np.sin(angle) * math.sqrt(2.0 / band)
        freq[2 * k - 1] = freq[2 * k] = k
    basis[band - 1] = (1.0 - 2.0 * (rows % 2)) / math.sqrt(band)
    freq[band - 1] = band // 2
    row_term = kappa_sq + 4.0 * np.sin(np.pi * freq / band) ** 2
    out = {}
    high, low = high_low(basis)
    out["row_forward"] = np.concatenate([high, high, low], 1)
    share = np.zeros((band, 16))
    for row, at in ((0, 0), (1, 1), (2, band - 2), (3, band - 1)):
        share[:, row] = prior_scale * basis[:, at]
    share[:, 8 + 1] = prior_scale * basis[:, 0]
    share[:, 8 + 2] = prior_scale * basis[:, band - 1]
    high, low = high_low(share)
    out["halo_forward"] = np.concatenate([high, high, low], 1)
    high, low = high_low(basis.T)
    out["row_inverse"] = np.concatenate([high, high, low], 1)
    out["row_term"] = np.tile(row_term[:, None], (1, lanes)).astype(np.float32)

    count = lanes // 2 + 1
    outer = np.arange(count)
    inner = np.arange(lanes)
    angle = 2.0 * np.pi * ((outer[:, None] * inner[None, :]) % lanes) / lanes
    section = np.zeros((2 * half, lanes))
    section[:count] = np.cos(angle)
    section[half : half + count] = np.sin(angle)
    high, low = high_low(section)
    out["outer_forward"] = np.concatenate([high, high, low], 1)
    section = section.T.copy()
    section[:, half:] *= -1.0
    high, low = high_low(section)
    out["outer_inverse"] = np.concatenate([high, high, low], 1)

    angle = 2.0 * np.pi * outer[:, None] * inner[None, :] / total_cols
    twist = np.zeros((2, half, lanes), np.float32)
    twist[0, :count] = np.cos(angle)
    twist[1, :count] = np.sin(angle)
    out["twist"] = twist

    kept_inner = np.concatenate([np.arange(kept // 2), np.arange(lanes - kept // 2, lanes)])
    angle = 2.0 * np.pi * ((inner[:, None] * kept_inner[None, :]) % lanes) / lanes
    cosine, sine = np.cos(angle), np.sin(angle)
    high, low = high_low(np.block([[cosine, -sine], [sine, cosine]]))
    out["inner_forward"] = np.concatenate([high, low], 1)
    high, low = high_low(np.block([[cosine.T, sine.T], [-sine.T, cosine.T]]))
    out["inner_inverse"] = np.concatenate([high, high, low], 0)

    col_freq = outer[:, None] + lanes * kept_inner[None, :]
    quarter = total_cols // 4
    retained = (col_freq < quarter) | (col_freq > total_cols - quarter)
    twice = np.where((outer == 0) | (outer == lanes // 2), 1.0, 2.0)[:, None]
    weight = np.zeros((half, 2 * kept))
    weight[:count] = np.tile(np.where(retained, twice / total_cols, 0.0), (1, 2))
    term = np.zeros((half, 2 * kept))
    term[:count] = np.tile(4.0 * np.sin(np.pi * col_freq / total_cols) ** 2, (1, 2))
    out["weight"] = weight.astype(np.float32)
    out["col_term"] = term.astype(np.float32)
    return out


def split(value):
    high = value.astype(jnp.bfloat16)
    low = (value - high.astype(jnp.float32)).astype(jnp.bfloat16)
    return high, low


def dot(left, right):
    return jnp.dot(left, right, preferred_element_type=jnp.float32)


def left_product(table, value):
    high, low = split(value)
    return dot(table, jnp.concatenate([high, low, high], 0))


def lane_index(shape):
    return lax.broadcasted_iota(jnp.int32, shape, 1)


def neighbours(field):
    full = field.shape[1]
    return pltpu.roll(field, 1, 1) + pltpu.roll(field, full - 1, 1)


def stencil(pad):
    full = width + lanes
    field = pad[8:72, :]
    near = pad[7:71, :] + pad[9:73, :]
    far = pad[6:70, :] + pad[10:74, :]
    across = neighbours(2.0 * near - (2.0 * centre) * field)
    distant = far + pltpu.roll(field, 2, 1) + pltpu.roll(field, full - 2, 1)
    return prior_scale * ((centre * centre + 4.0) * field - 2.0 * centre * near + across + distant)


def halo_terms(place, swap_a, swap_b, halo):
    even = place[0] % 2 == 0
    span = swap_a.shape[1]
    halo[...] = jnp.zeros((8, width + lanes), jnp.float32)
    halo[0:2, :span] = jnp.where(even, swap_b[...], swap_a[...])
    halo[2:4, :span] = jnp.where(even, swap_a[...], swap_b[...])
    rows = halo[...]
    beside = 2.0 * neighbours(rows) - (2.0 * centre) * rows
    return rows, beside


def halo_rows(rows, beside):
    return prior_scale * jnp.concatenate(
        [
            beside[1:2] + rows[0:1],
            rows[1:2],
            jnp.zeros((4, width + lanes), jnp.float32),
            rows[2:3],
            beside[2:3] + rows[3:4],
        ],
        0,
    )


def add_halo_rows(field, added):
    index = lax.broadcasted_iota(jnp.int32, added.shape, 0)
    return jnp.concatenate(
        [
            field[:8] + jnp.where(index < 4, added, 0.0),
            field[8 : band - 8],
            field[band - 8 :] + jnp.where(index >= 4, added, 0.0),
        ],
        0,
    )


def store_coefs(place, coefs, buffer, outs, count):
    target = outs[0] if len(outs) == 1 else buffer
    for part in range(parts):
        for tile in range(count):
            target[part, tile * lines : (tile + 1) * lines, :] = coefs[
                part * lines : (part + 1) * lines, tile * lanes : (tile + 1) * lanes
            ]
    store_blocks(place, buffer, outs)


def store_blocks(place, buffer, outs):
    if len(outs) == 1:
        return
    for mask, out in enumerate(outs):
        out[...] = buffer[place[1] ^ mask]


def load_blocks(place, refs, buffer):
    if len(refs) == 1:
        return refs[0]
    for mask, ref in enumerate(refs):
        buffer[place[1] ^ mask] = ref[...]
    return buffer


def load_coefs(buffer, count):
    return jnp.concatenate(
        [
            jnp.concatenate(
                [buffer[part, tile * lines : (tile + 1) * lines, :] for part in range(parts)], 0
            )
            for tile in range(count)
        ],
        1,
    )


def gradient_kernel(
    latent, counts, exposure, basis, coefs, grad, fisher, pad, counts_here, exposure_here, sems
):
    fields = ((latent, pad), (exposure, exposure_here), (counts, counts_here))
    copies = []
    for which, (there, here) in enumerate(fields):
        skip = 8 if which == 0 else 0
        for part in range(pieces):
            rows = pl.ds(part * (band // pieces), band // pieces)
            onto = pl.ds(part * (band // pieces) + skip, band // pieces)
            copies.append(
                pltpu.make_async_copy(
                    there.at[rows, :], here.at[onto, :width], sems.at[which, part]
                )
            )
            copies[-1].start()
    pad[0:8, :] = jnp.zeros((8, width + lanes), jnp.float32)
    pad[72:80, :] = jnp.zeros((8, width + lanes), jnp.float32)
    pad[8:72, width:] = jnp.zeros((band, lanes), jnp.float32)
    for copy in copies[:pieces]:
        copy.wait()
    prior = stencil(pad)
    for copy in copies[pieces:]:
        copy.wait()
    mean_rate = exposure_here[...].astype(jnp.float32) * jnp.exp(pad[8:72, :width])
    ratio = dispersion / (dispersion + mean_rate)
    fisher[...] = mean_rate * ratio
    score = (counts_here[...].astype(jnp.float32) - mean_rate) * ratio
    inside = score - prior[:, :width]
    grad[...] = inside
    coefs[...] = left_product(basis[...], jnp.concatenate([inside, -prior[:, width:]], 1))


def gradient_halo_kernel(place, coefs, swap_a, swap_b, basis, *rest):
    *outs, added, halo, buffer = rest
    rows, beside = halo_terms(place, swap_a, swap_b, halo)
    added[...] = -halo_rows(rows, beside)
    whole = coefs[...] - left_product(basis[...], jnp.concatenate([rows, beside], 0))
    spill = whole[:, width:]
    spill = spill + pltpu.roll(spill, lanes // 2, 1)
    store_coefs(place, jnp.concatenate([whole[:, :width], spill], 1), buffer, outs, tiles + 1)


def gather_lines(incoming, edges):
    lane = lane_index((tiles, lanes))
    sub = lax.broadcasted_iota(jnp.int32, (tiles, lanes), 0)
    first = (sub == 0) & (lane < 2)
    last = (sub == tiles - 1) & (lane >= lanes - 2)
    line_fields = []
    for line in range(lines):
        blocks = [
            incoming[part, pl.ds(line, tiles, stride=lines), :] for part in range(parts)
        ]
        if edges:
            spill = [
                incoming[part, tiles * lines + line : tiles * lines + line + 1, :]
                for part in range(parts)
            ]
            for part in range(parts):
                if part > 0:
                    blocks[part] = blocks[part] + jnp.where(first, spill[part - 1], 0.0)
                if part < parts - 1:
                    blocks[part] = blocks[part] + jnp.where(last, spill[part + 1], 0.0)
        line_fields.append(jnp.concatenate(blocks, 0))
    return jnp.concatenate(line_fields, 1)


def columns_forward(field, outer_forward, inner_forward, twist):
    section = left_product(outer_forward[...], field)
    cosine, sine = twist[0], twist[1]
    turned = []
    for line in range(lines):
        cols = slice(line * lanes, (line + 1) * lanes)
        even_part, odd_part = section[:half, cols], section[half:, cols]
        real = even_part * cosine - odd_part * sine
        imag = -(odd_part * cosine + even_part * sine)
        turned.append(jnp.concatenate([real, imag], 1))
    high, low = split(jnp.concatenate(turned, 0))
    both = dot(high, inner_forward[...])
    return both[:, : 2 * kept] + both[:, 2 * kept :] + dot(low, inner_forward[:, : 2 * kept])


def scale_spectrum(place, spectrum, row_term, col_term, weight):
    row_line = row_term[pl.ds(pl.multiple_of(place[1] * lines, lines), lines), :]
    scaled = []
    total = jnp.zeros((half, 2 * kept), jnp.float32)
    for line in range(lines):
        inner_term = row_line[line : line + 1, :] + col_term[...]
        quad = prior_scale * inner_term * inner_term
        gain = -quad / (quad + weight_shift) * weight[...]
        piece = spectrum[line * half : (line + 1) * half, :]
        scaled.append(piece * gain)
        total = total + piece * scaled[-1]
    return jnp.concatenate(scaled, 0), total


def columns_inverse(scaled, outer_inverse, inner_inverse, twist):
    high, low = split(scaled)
    back = dot(jnp.concatenate([high, low], 1), inner_inverse[: 4 * kept, :]) + dot(
        high, inner_inverse[4 * kept :, :]
    )
    cosine, sine = twist[0], twist[1]
    reals, imags = [], []
    for line in range(lines):
        rows = slice(line * half, (line + 1) * half)
        real, imag = back[rows, :lanes], back[rows, lanes:]
        reals.append(real * cosine - imag * sine)
        imags.append(imag * cosine + real * sine)
    folded = jnp.concatenate([jnp.concatenate(reals, 1), jnp.concatenate(imags, 1)], 0)
    return left_product(outer_inverse[...], folded)


def store_lines(result, out):
    for line in range(lines):
        for part in range(parts):
            out[part, pl.ds(line, tiles, stride=lines), :] = result[
                part * tiles : (part + 1) * tiles, line * lanes : (line + 1) * lanes
            ]


def filter_kernel(place, *rest):
    blocks_in, rest = rest[:parts], rest[parts:]
    row_term, col_term, weight, outer_forward, inner_forward, twist, outer_inverse, inner_inverse = (
        rest[:8]
    )
    blocks_out, (incoming, out) = rest[8 : 8 + parts], rest[8 + parts :]
    incoming = load_blocks(place, blocks_in, incoming)
    field = gather_lines(incoming, True)
    spectrum = columns_forward(field, outer_forward, inner_forward, twist)
    scaled, _ = scale_spectrum(place, spectrum, row_term, col_term, weight)
    result = columns_inverse(scaled, outer_inverse, inner_inverse, twist)
    store_lines(result, out)
    edge_lane = lane_index((1, lanes))
    nothing = jnp.zeros((1, lanes), jnp.float32)
    for line in range(lines):
        cols = slice(line * lanes, (line + 1) * lanes)
        spot = tiles * lines + line
        for part in range(parts):
            after, before, from_left, from_right = nothing, nothing, nothing, nothing
            if part < parts - 1:
                row = slice((part + 1) * tiles, (part + 1) * tiles + 1)
                after = result[row, cols] + field[row, cols]
                from_right = incoming[part + 1, spot : spot + 1, :]
            if part > 0:
                row = slice(part * tiles - 1, part * tiles)
                before = result[row, cols] + field[row, cols]
                from_left = incoming[part - 1, spot : spot + 1, :]
            middle = jnp.where(edge_lane >= lanes // 2, from_left, from_right)
            out[part, spot : spot + 1, :] = jnp.where(
                edge_lane < 2, after, jnp.where(edge_lane >= lanes - 2, before, middle)
            )
    store_blocks(place, out, blocks_out)


def front_kernel(place, *rest):
    blocks_in, rest = rest[:parts], rest[parts:]
    sums, row_term, col_term, weight, outer_forward, inner_forward, twist = rest[:7]
    spectrum_out, known, incoming = rest[7:]
    incoming = load_blocks(place, blocks_in, incoming)
    field = gather_lines(incoming, False)
    spectrum = columns_forward(field, outer_forward, inner_forward, twist)
    scaled, total = scale_spectrum(place, spectrum, row_term, col_term, weight)
    spectrum_out[...] = scaled
    energy = jnp.sum(total, axis=(0, 1), keepdims=True)
    line = sums[...] + jnp.where(lane_index((1, lanes)) == 2, energy, 0.0)
    for part in range(parts):
        known[part] = line


def back_kernel(scaled, twist, outer_inverse, inner_inverse, out):
    store_lines(columns_inverse(scaled[...], outer_inverse, inner_inverse, twist), out)


def search_kernel(place, *rest):
    *blocks, grad, added, basis, full_grad, search, send_a, send_b, buffer = rest
    even = place[0] % 2 == 0
    buffer = load_blocks(place, blocks, buffer)
    update = left_product(basis[...], load_coefs(buffer, tiles + 1))
    beyond = update[:, width:]
    spill = pltpu.roll(beyond, lanes // 2, 1)
    lane = lane_index((band, lanes))
    base = add_halo_rows(grad[...], added[:, :width])
    head = base[:, :lanes] + jnp.where(lane < 2, spill, 0.0)
    tail = base[:, width - lanes :] + jnp.where(lane >= lanes - 2, spill, 0.0)
    whole = jnp.concatenate([head, base[:, lanes : width - lanes], tail], 1)
    full_grad[...] = whole
    found = jnp.concatenate([whole + update[:, :width], beyond], 1)
    search[...] = found
    top, bottom = found[:2, :], found[band - 2 :, :]
    send_a[...] = jnp.where(even, bottom, top)
    send_b[...] = jnp.where(even, top, bottom)


def image_kernel(search, fisher, basis, coefs, image, pad):
    pad[0:8, :] = jnp.zeros((8, width + lanes), jnp.float32)
    pad[72:80, :] = jnp.zeros((8, width + lanes), jnp.float32)
    pad[8:72, :] = search[...]
    result = stencil(pad)[:, :width] + fisher[...] * search[:, :width]
    image[...] = result
    coefs[...] = left_product(basis[...], result)


def image_halo_kernel(place, coefs, swap_a, swap_b, basis, *rest):
    *outs, added, halo, buffer = rest
    rows, beside = halo_terms(place, swap_a, swap_b, halo)
    added[...] = halo_rows(rows, beside)
    both = jnp.concatenate([rows, beside], 0)[:, :width]
    store_coefs(place, coefs[...] + left_product(basis[...], both), buffer, outs, tiles)


def sums_kernel(search, grad, partial, added, image, sums):
    field = search[:, :width]
    result = add_halo_rows(partial[...], added[:, :width])
    image[...] = result
    products = (grad[...] * field, field * result, result * result)
    lane = lane_index((1, lanes))
    line = jnp.zeros((1, lanes), jnp.float32)
    for which, product in enumerate(products):
        total = jnp.sum(product, axis=(0, 1), keepdims=True)
        line = line + jnp.where(lane == which, total, 0.0)
    sums[...] = line


def second_kernel(place, *rest):
    *blocks, image, basis, second, buffer = rest
    buffer = load_blocks(place, blocks, buffer)
    second[...] = image[...] + left_product(basis[...], load_coefs(buffer, tiles))


def final_kernel(
    sums, search, grad, image, second, step, residual, direction, step_here, residual_here, direction_here, sems
):
    total = jnp.sum(sums[...], axis=0)
    first_product = total[0:1, 0:1]
    curvature = total[0:1, 1:2]
    image_product = total[0:1, 2:3]
    step_size = first_product / curvature
    ratio = step_size * (image_product / curvature) - 1.0
    copies = []
    for part in range(pieces):
        rows = slice(part * (band // pieces), (part + 1) * (band // pieces))
        field = search[rows, :width]
        results = (
            (step_size * field, step_here, step),
            (grad[rows, :] - step_size * image[rows, :], residual_here, residual),
            ((field - step_size * second[rows, :]) + ratio * field, direction_here, direction),
        )
        for which, (value, here, there) in enumerate(results):
            here[rows, :] = value
            copies.append(
                pltpu.make_async_copy(here.at[rows, :], there.at[rows, :], sems.at[which, part])
            )
            copies[-1].start()
    for copy in copies:
        copy.wait()


def call(kernel, shapes, args, scratch=(), flops=0, far=0, far_out=False):
    in_specs = [
        pl.BlockSpec(memory_space=pltpu.HBM if i < far else pltpu.VMEM) for i in range(len(args))
    ]
    if args[0].ndim == 1:
        in_specs[0] = pl.BlockSpec(memory_space=pltpu.SMEM)
    outs = tuple(jax.ShapeDtypeStruct(s, jnp.float32) for s in shapes)
    moved = 4 * (sum(a.size for a in args) + sum(o.size for o in outs))
    return pl.pallas_call(
        kernel,
        out_shape=outs,
        in_specs=in_specs,
        out_specs=tuple(
            pl.BlockSpec(memory_space=pltpu.HBM if far_out else pltpu.VMEM) for _ in outs
        ),
        scratch_shapes=list(scratch),
        compiler_params=pltpu.CompilerParams(vmem_limit_bytes=vmem_bytes),
        cost_estimate=pl.CostEstimate(flops=flops, bytes_accessed=moved, transcendentals=0),
    )(*args)


def row_swaps():
    count = lax.axis_size("rows")
    inner = [(i, i ^ 1) for i in range(count)]
    outer = [(i, i + 1) for i in range(1, count - 1, 2)] + [(i + 1, i) for i in range(1, count - 1, 2)]
    return inner, outer


def exchange(blocks):
    if len(blocks) == 1:
        return [lax.all_to_all(blocks[0], "cols", split_axis=0, concat_axis=0, tiled=True)]
    count = lax.axis_size("cols")
    got = {}
    for mask in (4, 3, 5, 2, 6, 1, 7):
        got[mask] = lax.ppermute(blocks[mask], "cols", [(i, i ^ mask) for i in range(count)])
    return [blocks[0]] + [got[mask] for mask in range(1, parts)]


def swap_rows(send_a, send_b):
    inner, outer = row_swaps()
    return lax.ppermute(send_a, "rows", inner), lax.ppermute(send_b, "rows", outer)


def row_swap(value, mask):
    count = lax.axis_size("rows")
    return lax.ppermute(value, "rows", [(i, i ^ mask) for i in range(count)])


def on_device(latent, counts, exposure):
    consts = tables()
    tab = {name: jnp.asarray(value) for name, value in consts.items()}
    row_index = lax.axis_index("rows")
    place = jnp.stack([row_index, lax.axis_index("cols")]).astype(jnp.int32)
    full = width + lanes
    pad = pltpu.VMEM((80, full), jnp.float32)
    halo = pltpu.VMEM((8, full), jnp.float32)
    wide = ((tiles + 1) * lines, lanes)
    slim = (tiles * lines, lanes)
    wide_buffer = pltpu.VMEM((parts, *wide), jnp.float32)
    slim_buffer = pltpu.VMEM((parts, *slim), jnp.float32)
    block = (band, width)
    extended = (band, full)
    forward = [
        tab[name]
        for name in ("row_term", "col_term", "weight", "outer_forward", "inner_forward", "twist")
    ]
    inverse = [tab["outer_inverse"], tab["inner_inverse"]]

    even = row_index % 2 == 0
    top, bottom = latent[:2], latent[band - 2 :]
    swap_a, swap_b = swap_rows(jnp.where(even, bottom, top), jnp.where(even, top, bottom))
    coefs, grad_part, fisher = call(
        gradient_kernel,
        (extended, block, block),
        (
            *(pltpu.with_memory_space_constraint(a, pltpu.HBM) for a in (latent, counts, exposure)),
            tab["row_forward"],
        ),
        (
            pad,
            pltpu.VMEM(block, jnp.int32),
            pltpu.VMEM(block, jnp.int32),
            pltpu.SemaphoreType.DMA((3, pieces)),
        ),
        flops=10**9,
        far=3,
    )
    *blocks, added = call(
        gradient_halo_kernel,
        (wide,) * parts + ((8, full),),
        (place, coefs, swap_a, swap_b, tab["halo_forward"]),
        (halo, wide_buffer),
        flops=10**7,
    )
    blocks = exchange(blocks)
    blocks = call(
        filter_kernel,
        (wide,) * parts,
        (place, *blocks, *forward, *inverse),
        (wide_buffer, wide_buffer),
        flops=10**9,
    )
    blocks = exchange(blocks)
    grad, search, send_a, send_b = call(
        search_kernel,
        (block, extended, (2, full), (2, full)),
        (place, *blocks, grad_part, added, tab["row_inverse"]),
        (wide_buffer,),
        flops=10**8,
    )
    swap_a, swap_b = swap_rows(send_a, send_b)
    coefs, partial = call(
        image_kernel,
        (block, block),
        (search, fisher, tab["row_forward"]),
        (pad,),
        flops=10**9,
    )
    *blocks, added = call(
        image_halo_kernel,
        (slim,) * parts + ((8, full),),
        (place, coefs, swap_a, swap_b, tab["halo_forward"]),
        (halo, slim_buffer),
        flops=10**7,
    )
    blocks = exchange(blocks)
    image, sums = call(
        sums_kernel, (block, (1, lanes)), (search, grad, partial, added), flops=10**8
    )
    scaled, known = call(
        front_kernel,
        ((lines * half, 2 * kept), (parts, 1, lanes)),
        (place, *blocks, sums, *forward),
        (slim_buffer,),
        flops=10**8,
    )
    (block_out,) = call(
        back_kernel, ((parts, *slim),), (scaled, tab["twist"], *inverse), flops=10**9
    )
    block_out, known = lax.optimization_barrier((block_out, known + row_swap(known, 1)))
    blocks = exchange([block_out])
    known = known + row_swap(known, 2) + row_swap(known, 4) + row_swap(known, 6)
    known = known + row_swap(known, 8) + row_swap(known, 16) + row_swap(known, 24)
    sums = exchange([known])[0]
    (second,) = call(
        second_kernel,
        (block,),
        (place, *blocks, image, tab["row_inverse"]),
        (slim_buffer,),
        flops=10**8,
    )
    return call(
        final_kernel,
        (block, block, block),
        (sums, search, grad, image, second),
        (pltpu.VMEM(block, jnp.float32),) * 3 + (pltpu.SemaphoreType.DMA((3, pieces)),),
        flops=10**6,
        far_out=True,
    )


def solution(mesh):
    placed = (P("rows", "cols"), P("rows", "cols"), P("rows", "cols"))
    return jax.shard_map(
        on_device,
        mesh=mesh,
        in_specs=placed,
        out_specs=placed,
        check_vma=False,
    )
```

```python
import functools
import math

import jax
import jax.numpy as jnp
import ml_dtypes
import numpy as np
from jax import lax
from jax.experimental import pallas as pl
from jax.experimental.pallas import tpu as pltpu
from jax.sharding import PartitionSpec as P

dispersion = 4.0
prior_scale = 0.25
kappa_sq = 0.05
weight_shift = 1.0
centre = kappa_sq + 4.0

band = 64
width = 2048
lanes = 128
tiles = width // lanes
parts = 8
total_cols = width * parts
lines = band // parts
half = 72
kept = 64
vmem_bytes = 48 * 1024 * 1024
pieces = 4
pairwise = (True, True, True, False)


def high_low(table):
    high = table.astype(ml_dtypes.bfloat16)
    low = (table - high.astype(np.float64)).astype(ml_dtypes.bfloat16)
    return high, low


@functools.cache
def tables():
    rows = np.arange(band)
    freq = np.zeros(band)
    basis = np.zeros((band, band))
    basis[0] = 1.0 / math.sqrt(band)
    for k in range(1, band // 2):
        angle = 2.0 * np.pi * ((k * rows) % band) / band
        basis[2 * k - 1] = np.cos(angle) * math.sqrt(2.0 / band)
        basis[2 * k] = np.sin(angle) * math.sqrt(2.0 / band)
        freq[2 * k - 1] = freq[2 * k] = k
    basis[band - 1] = (1.0 - 2.0 * (rows % 2)) / math.sqrt(band)
    freq[band - 1] = band // 2
    row_term = kappa_sq + 4.0 * np.sin(np.pi * freq / band) ** 2
    out = {}
    high, low = high_low(basis)
    out["row_forward"] = np.concatenate([high, high, low], 1)
    share = np.zeros((band, 16))
    for row, at in ((0, 0), (1, 1), (2, band - 2), (3, band - 1)):
        share[:, row] = prior_scale * basis[:, at]
    share[:, 8 + 1] = prior_scale * basis[:, 0]
    share[:, 8 + 2] = prior_scale * basis[:, band - 1]
    high, low = high_low(share)
    out["halo_forward"] = np.concatenate([high, high, low], 1)
    high, low = high_low(basis.T)
    out["row_inverse"] = np.concatenate([high, high, low], 1)
    out["row_term"] = np.tile(row_term[:, None], (1, lanes)).astype(np.float32)

    count = lanes // 2 + 1
    outer = np.arange(count)
    inner = np.arange(lanes)
    angle = 2.0 * np.pi * ((outer[:, None] * inner[None, :]) % lanes) / lanes
    section = np.zeros((2 * half, lanes))
    section[:count] = np.cos(angle)
    section[half : half + count] = np.sin(angle)
    high, low = high_low(section)
    out["outer_forward"] = np.concatenate([high, high, low], 1)
    section = section.T.copy()
    section[:, half:] *= -1.0
    high, low = high_low(section)
    out["outer_inverse"] = np.concatenate([high, high, low], 1)

    angle = 2.0 * np.pi * outer[:, None] * inner[None, :] / total_cols
    twist = np.zeros((2, half, lanes), np.float32)
    twist[0, :count] = np.cos(angle)
    twist[1, :count] = np.sin(angle)
    out["twist"] = twist

    kept_inner = np.concatenate([np.arange(kept // 2), np.arange(lanes - kept // 2, lanes)])
    angle = 2.0 * np.pi * ((inner[:, None] * kept_inner[None, :]) % lanes) / lanes
    cosine, sine = np.cos(angle), np.sin(angle)
    high, low = high_low(np.block([[cosine, -sine], [sine, cosine]]))
    out["inner_forward"] = np.concatenate([high, low], 1)
    high, low = high_low(np.block([[cosine.T, sine.T], [-sine.T, cosine.T]]))
    out["inner_inverse"] = np.concatenate([high, high, low], 0)

    col_freq = outer[:, None] + lanes * kept_inner[None, :]
    quarter = total_cols // 4
    retained = (col_freq < quarter) | (col_freq > total_cols - quarter)
    twice = np.where((outer == 0) | (outer == lanes // 2), 1.0, 2.0)[:, None]
    weight = np.zeros((half, 2 * kept))
    weight[:count] = np.tile(np.where(retained, twice / total_cols, 0.0), (1, 2))
    term = np.zeros((half, 2 * kept))
    term[:count] = np.tile(4.0 * np.sin(np.pi * col_freq / total_cols) ** 2, (1, 2))
    out["weight"] = weight.astype(np.float32)
    out["col_term"] = term.astype(np.float32)
    return out


def split(value):
    high = value.astype(jnp.bfloat16)
    low = (value - high.astype(jnp.float32)).astype(jnp.bfloat16)
    return high, low


def dot(left, right):
    return jnp.dot(left, right, preferred_element_type=jnp.float32)


def left_product(table, value):
    high, low = split(value)
    return dot(table, jnp.concatenate([high, low, high], 0))


def lane_index(shape):
    return lax.broadcasted_iota(jnp.int32, shape, 1)


def neighbours(field):
    full = field.shape[1]
    return pltpu.roll(field, 1, 1) + pltpu.roll(field, full - 1, 1)


def stencil(pad):
    full = width + lanes
    field = pad[8:72, :]
    near = pad[7:71, :] + pad[9:73, :]
    far = pad[6:70, :] + pad[10:74, :]
    across = neighbours(2.0 * near - (2.0 * centre) * field)
    distant = far + pltpu.roll(field, 2, 1) + pltpu.roll(field, full - 2, 1)
    return prior_scale * ((centre * centre + 4.0) * field - 2.0 * centre * near + across + distant)


def halo_terms(place, swap_a, swap_b, halo):
    even = place[0] % 2 == 0
    span = swap_a.shape[1]
    halo[...] = jnp.zeros((8, width + lanes), jnp.float32)
    halo[0:2, :span] = jnp.where(even, swap_b[...], swap_a[...])
    halo[2:4, :span] = jnp.where(even, swap_a[...], swap_b[...])
    rows = halo[...]
    beside = 2.0 * neighbours(rows) - (2.0 * centre) * rows
    return rows, beside


def halo_rows(rows, beside):
    return prior_scale * jnp.concatenate(
        [
            beside[1:2] + rows[0:1],
            rows[1:2],
            jnp.zeros((4, width + lanes), jnp.float32),
            rows[2:3],
            beside[2:3] + rows[3:4],
        ],
        0,
    )


def add_halo_rows(field, added):
    index = lax.broadcasted_iota(jnp.int32, added.shape, 0)
    return jnp.concatenate(
        [
            field[:8] + jnp.where(index < 4, added, 0.0),
            field[8 : band - 8],
            field[band - 8 :] + jnp.where(index >= 4, added, 0.0),
        ],
        0,
    )


def store_coefs(place, coefs, buffer, outs, count):
    target = outs[0] if len(outs) == 1 else buffer
    for part in range(parts):
        for tile in range(count):
            target[part, tile * lines : (tile + 1) * lines, :] = coefs[
                part * lines : (part + 1) * lines, tile * lanes : (tile + 1) * lanes
            ]
    store_blocks(place, buffer, outs)


def store_blocks(place, buffer, outs):
    if len(outs) == 1:
        return
    for mask, out in enumerate(outs):
        out[...] = buffer[place[1] ^ mask]


def load_blocks(place, refs, buffer):
    if len(refs) == 1:
        return refs[0]
    for mask, ref in enumerate(refs):
        buffer[place[1] ^ mask] = ref[...]
    return buffer


def load_coefs(buffer, count):
    return jnp.concatenate(
        [
            jnp.concatenate(
                [buffer[part, tile * lines : (tile + 1) * lines, :] for part in range(parts)], 0
            )
            for tile in range(count)
        ],
        1,
    )


def gradient_kernel(
    latent, counts, exposure, basis, coefs, grad, fisher, pad, counts_here, exposure_here, sems
):
    fields = ((latent, pad), (exposure, exposure_here), (counts, counts_here))
    copies = []
    for which, (there, here) in enumerate(fields):
        skip = 8 if which == 0 else 0
        for part in range(pieces):
            rows = pl.ds(part * (band // pieces), band // pieces)
            onto = pl.ds(part * (band // pieces) + skip, band // pieces)
            copies.append(
                pltpu.make_async_copy(
                    there.at[rows, :], here.at[onto, :width], sems.at[which, part]
                )
            )
            copies[-1].start()
    pad[0:8, :] = jnp.zeros((8, width + lanes), jnp.float32)
    pad[72:80, :] = jnp.zeros((8, width + lanes), jnp.float32)
    pad[8:72, width:] = jnp.zeros((band, lanes), jnp.float32)
    for copy in copies[:pieces]:
        copy.wait()
    prior = stencil(pad)
    for copy in copies[pieces:]:
        copy.wait()
    mean_rate = exposure_here[...].astype(jnp.float32) * jnp.exp(pad[8:72, :width])
    ratio = dispersion / (dispersion + mean_rate)
    fisher[...] = mean_rate * ratio
    score = (counts_here[...].astype(jnp.float32) - mean_rate) * ratio
    inside = score - prior[:, :width]
    grad[...] = inside
    coefs[...] = left_product(basis[...], jnp.concatenate([inside, -prior[:, width:]], 1))


def gradient_halo_kernel(place, coefs, swap_a, swap_b, basis, *rest):
    *outs, added, halo, buffer = rest
    rows, beside = halo_terms(place, swap_a, swap_b, halo)
    added[...] = -halo_rows(rows, beside)
    whole = coefs[...] - left_product(basis[...], jnp.concatenate([rows, beside], 0))
    spill = whole[:, width:]
    spill = spill + pltpu.roll(spill, lanes // 2, 1)
    store_coefs(place, jnp.concatenate([whole[:, :width], spill], 1), buffer, outs, tiles + 1)


def filter_kernel(place, *rest, edges, taken, given):
    blocks_in, rest = rest[:taken], rest[taken:]
    (
        sums,
        row_term,
        col_term,
        weight,
        outer_forward,
        outer_inverse,
        inner_forward,
        inner_inverse,
        twist,
    ) = rest[:9]
    blocks_out, (incoming, out) = rest[9 : 9 + given], rest[9 + given :]
    incoming = load_blocks(place, blocks_in, incoming)
    if given == 1:
        out = blocks_out[0]
    lane = lane_index((tiles, lanes))
    sub = lax.broadcasted_iota(jnp.int32, (tiles, lanes), 0)
    first = (sub == 0) & (lane < 2)
    last = (sub == tiles - 1) & (lane >= lanes - 2)
    line_fields = []
    for line in range(lines):
        blocks = [
            incoming[part, pl.ds(line, tiles, stride=lines), :] for part in range(parts)
        ]
        if edges:
            spill = [
                incoming[part, tiles * lines + line : tiles * lines + line + 1, :]
                for part in range(parts)
            ]
            for part in range(parts):
                if part > 0:
                    blocks[part] = blocks[part] + jnp.where(first, spill[part - 1], 0.0)
                if part < parts - 1:
                    blocks[part] = blocks[part] + jnp.where(last, spill[part + 1], 0.0)
        line_fields.append(jnp.concatenate(blocks, 0))
    field = jnp.concatenate(line_fields, 1)
    section = left_product(outer_forward[...], field)
    cosine, sine = twist[0], twist[1]
    turned = []
    for line in range(lines):
        cols = slice(line * lanes, (line + 1) * lanes)
        even_part, odd_part = section[:half, cols], section[half:, cols]
        real = even_part * cosine - odd_part * sine
        imag = -(odd_part * cosine + even_part * sine)
        turned.append(jnp.concatenate([real, imag], 1))
    high, low = split(jnp.concatenate(turned, 0))
    both = dot(high, inner_forward[...])
    spectrum = both[:, : 2 * kept] + both[:, 2 * kept :] + dot(low, inner_forward[:, : 2 * kept])
    row_line = row_term[pl.ds(pl.multiple_of(place[1] * lines, lines), lines), :]
    scaled = []
    total = jnp.zeros((half, 2 * kept), jnp.float32)
    for line in range(lines):
        inner_term = row_line[line : line + 1, :] + col_term[...]
        quad = prior_scale * inner_term * inner_term
        gain = -quad / (quad + weight_shift) * weight[...]
        piece = spectrum[line * half : (line + 1) * half, :]
        scaled.append(piece * gain)
        if not edges:
            total = total + piece * scaled[-1]
    if not edges:
        energy = jnp.sum(total, axis=(0, 1), keepdims=True)
        third = lax.broadcasted_iota(jnp.int32, (8, lanes), 0) == 2
        known = sums[...] + jnp.where(third, energy, 0.0)
        for part in range(parts):
            out[part, tiles * lines :, :] = known
    high, low = split(jnp.concatenate(scaled, 0))
    back = dot(jnp.concatenate([high, low], 1), inner_inverse[: 4 * kept, :]) + dot(
        high, inner_inverse[4 * kept :, :]
    )
    reals, imags = [], []
    for line in range(lines):
        rows = slice(line * half, (line + 1) * half)
        real, imag = back[rows, :lanes], back[rows, lanes:]
        reals.append(real * cosine - imag * sine)
        imags.append(imag * cosine + real * sine)
    folded = jnp.concatenate([jnp.concatenate(reals, 1), jnp.concatenate(imags, 1)], 0)
    result = left_product(outer_inverse[...], folded)
    edge_lane = lane_index((1, lanes))
    nothing = jnp.zeros((1, lanes), jnp.float32)
    for line in range(lines):
        cols = slice(line * lanes, (line + 1) * lanes)
        for part in range(parts):
            out[part, pl.ds(line, tiles, stride=lines), :] = result[
                part * tiles : (part + 1) * tiles, cols
            ]
        if edges:
            spot = tiles * lines + line
            for part in range(parts):
                after, before, from_left, from_right = nothing, nothing, nothing, nothing
                if part < parts - 1:
                    row = slice((part + 1) * tiles, (part + 1) * tiles + 1)
                    after = result[row, cols] + field[row, cols]
                    from_right = incoming[part + 1, spot : spot + 1, :]
                if part > 0:
                    row = slice(part * tiles - 1, part * tiles)
                    before = result[row, cols] + field[row, cols]
                    from_left = incoming[part - 1, spot : spot + 1, :]
                middle = jnp.where(edge_lane >= lanes // 2, from_left, from_right)
                out[part, spot : spot + 1, :] = jnp.where(
                    edge_lane < 2, after, jnp.where(edge_lane >= lanes - 2, before, middle)
                )
    store_blocks(place, out, blocks_out)


def search_kernel(place, *rest):
    *blocks, grad, added, basis, full_grad, search, send_a, send_b, buffer = rest
    even = place[0] % 2 == 0
    buffer = load_blocks(place, blocks, buffer)
    update = left_product(basis[...], load_coefs(buffer, tiles + 1))
    beyond = update[:, width:]
    spill = pltpu.roll(beyond, lanes // 2, 1)
    lane = lane_index((band, lanes))
    base = add_halo_rows(grad[...], added[:, :width])
    head = base[:, :lanes] + jnp.where(lane < 2, spill, 0.0)
    tail = base[:, width - lanes :] + jnp.where(lane >= lanes - 2, spill, 0.0)
    whole = jnp.concatenate([head, base[:, lanes : width - lanes], tail], 1)
    full_grad[...] = whole
    found = jnp.concatenate([whole + update[:, :width], beyond], 1)
    search[...] = found
    top, bottom = found[:2, :], found[band - 2 :, :]
    send_a[...] = jnp.where(even, bottom, top)
    send_b[...] = jnp.where(even, top, bottom)


def image_kernel(search, fisher, basis, coefs, image, pad):
    pad[0:8, :] = jnp.zeros((8, width + lanes), jnp.float32)
    pad[72:80, :] = jnp.zeros((8, width + lanes), jnp.float32)
    pad[8:72, :] = search[...]
    result = stencil(pad)[:, :width] + fisher[...] * search[:, :width]
    image[...] = result
    coefs[...] = left_product(basis[...], result)


def image_halo_kernel(place, coefs, swap_a, swap_b, basis, *rest):
    *outs, added, halo, buffer = rest
    rows, beside = halo_terms(place, swap_a, swap_b, halo)
    added[...] = halo_rows(rows, beside)
    both = jnp.concatenate([rows, beside], 0)[:, :width]
    store_coefs(place, coefs[...] + left_product(basis[...], both), buffer, outs, tiles)


def sums_kernel(search, grad, partial, added, image, sums):
    field = search[:, :width]
    result = add_halo_rows(partial[...], added[:, :width])
    image[...] = result
    products = (grad[...] * field, field * result, result * result)
    for row, product in enumerate(products):
        total = jnp.sum(product, axis=(0, 1), keepdims=True)
        sums[row : row + 1, :] = jnp.broadcast_to(total, (1, lanes))
    sums[3:8, :] = jnp.zeros((5, lanes), jnp.float32)


def spread_kernel(block, spread):
    total = block[0, tiles * lines :, :]
    for part in range(1, parts):
        total = total + block[part, tiles * lines :, :]
    lane = lane_index((1, lanes))
    line = jnp.where(lane == 0, total[0:1], jnp.where(lane == 1, total[1:2], total[2:3]))
    for row in range(spread.shape[0]):
        spread[row] = line


def second_kernel(block, image, basis, second):
    second[...] = image[...] + left_product(basis[...], load_coefs(block, tiles))


def final_kernel(
    sums, search, grad, image, second, step, residual, direction, step_here, residual_here, direction_here, sems
):
    total = jnp.sum(sums[...], axis=0)
    first_product = total[0:1, 0:1]
    curvature = total[0:1, 1:2]
    image_product = total[0:1, 2:3]
    step_size = first_product / curvature
    ratio = step_size * (image_product / curvature) - 1.0
    copies = []
    for part in range(pieces):
        rows = slice(part * (band // pieces), (part + 1) * (band // pieces))
        field = search[rows, :width]
        results = (
            (step_size * field, step_here, step),
            (grad[rows, :] - step_size * image[rows, :], residual_here, residual),
            ((field - step_size * second[rows, :]) + ratio * field, direction_here, direction),
        )
        for which, (value, here, there) in enumerate(results):
            here[rows, :] = value
            copies.append(
                pltpu.make_async_copy(here.at[rows, :], there.at[rows, :], sems.at[which, part])
            )
            copies[-1].start()
    for copy in copies:
        copy.wait()


def call(kernel, shapes, args, scratch=(), flops=0, far=0, far_out=False):
    in_specs = [
        pl.BlockSpec(memory_space=pltpu.HBM if i < far else pltpu.VMEM) for i in range(len(args))
    ]
    if args[0].ndim == 1:
        in_specs[0] = pl.BlockSpec(memory_space=pltpu.SMEM)
    outs = tuple(jax.ShapeDtypeStruct(s, jnp.float32) for s in shapes)
    moved = 4 * (sum(a.size for a in args) + sum(o.size for o in outs))
    return pl.pallas_call(
        kernel,
        out_shape=outs,
        in_specs=in_specs,
        out_specs=tuple(
            pl.BlockSpec(memory_space=pltpu.HBM if far_out else pltpu.VMEM) for _ in outs
        ),
        scratch_shapes=list(scratch),
        compiler_params=pltpu.CompilerParams(vmem_limit_bytes=vmem_bytes),
        cost_estimate=pl.CostEstimate(flops=flops, bytes_accessed=moved, transcendentals=0),
    )(*args)


def row_swaps():
    count = lax.axis_size("rows")
    inner = [(i, i ^ 1) for i in range(count)]
    outer = [(i, i + 1) for i in range(1, count - 1, 2)] + [(i + 1, i) for i in range(1, count - 1, 2)]
    return inner, outer


def exchange(blocks):
    if len(blocks) == 1:
        return [lax.all_to_all(blocks[0], "cols", split_axis=0, concat_axis=0, tiled=True)]
    count = lax.axis_size("cols")
    got = {}
    for mask in (4, 3, 5, 2, 6, 1, 7):
        got[mask] = lax.ppermute(blocks[mask], "cols", [(i, i ^ mask) for i in range(count)])
    return [blocks[0]] + [got[mask] for mask in range(1, parts)]


def swap_rows(send_a, send_b):
    inner, outer = row_swaps()
    return lax.ppermute(send_a, "rows", inner), lax.ppermute(send_b, "rows", outer)


def on_device(latent, counts, exposure):
    consts = tables()
    tab = {name: jnp.asarray(value) for name, value in consts.items()}
    row_index = lax.axis_index("rows")
    place = jnp.stack([row_index, lax.axis_index("cols")]).astype(jnp.int32)
    full = width + lanes
    pad = pltpu.VMEM((80, full), jnp.float32)
    halo = pltpu.VMEM((8, full), jnp.float32)
    wide = ((tiles + 1) * lines, lanes)
    slim = (tiles * lines, lanes)
    wide_buffer = pltpu.VMEM((parts, *wide), jnp.float32)
    slim_buffer = pltpu.VMEM((parts, *slim), jnp.float32)
    def sent(shape, pairwise):
        return (shape,) * parts if pairwise else ((parts, *shape),)

    block = (band, width)
    extended = (band, full)
    filters = [
        tab[name]
        for name in (
            "row_term",
            "col_term",
            "weight",
            "outer_forward",
            "outer_inverse",
            "inner_forward",
            "inner_inverse",
            "twist",
        )
    ]

    even = row_index % 2 == 0
    top, bottom = latent[:2], latent[band - 2 :]
    swap_a, swap_b = swap_rows(jnp.where(even, bottom, top), jnp.where(even, top, bottom))
    coefs, grad_part, fisher = call(
        gradient_kernel,
        (extended, block, block),
        (
            *(pltpu.with_memory_space_constraint(a, pltpu.HBM) for a in (latent, counts, exposure)),
            tab["row_forward"],
        ),
        (
            pad,
            pltpu.VMEM(block, jnp.int32),
            pltpu.VMEM(block, jnp.int32),
            pltpu.SemaphoreType.DMA((3, pieces)),
        ),
        flops=10**9,
        far=3,
    )
    *blocks, added = call(
        gradient_halo_kernel,
        sent(wide, pairwise[0]) + ((8, full),),
        (place, coefs, swap_a, swap_b, tab["halo_forward"]),
        (halo, wide_buffer),
        flops=10**7,
    )
    blocks = exchange(blocks)
    blocks = call(
        functools.partial(
            filter_kernel, edges=True, taken=len(blocks), given=parts if pairwise[1] else 1
        ),
        sent(wide, pairwise[1]),
        (place, *blocks, jnp.zeros((8, lanes), jnp.float32), *filters),
        (wide_buffer, wide_buffer),
        flops=10**9,
    )
    blocks = exchange(blocks)
    grad, search, send_a, send_b = call(
        search_kernel,
        (block, extended, (2, full), (2, full)),
        (place, *blocks, grad_part, added, tab["row_inverse"]),
        (wide_buffer,),
        flops=10**8,
    )
    swap_a, swap_b = swap_rows(send_a, send_b)
    coefs, partial = call(
        image_kernel,
        (block, block),
        (search, fisher, tab["row_forward"]),
        (pad,),
        flops=10**9,
    )
    *blocks, added = call(
        image_halo_kernel,
        sent(slim, pairwise[2]) + ((8, full),),
        (place, coefs, swap_a, swap_b, tab["halo_forward"]),
        (halo, slim_buffer),
        flops=10**7,
    )
    blocks = exchange(blocks)
    image, sums = call(
        sums_kernel, (block, (8, lanes)), (search, grad, partial, added), flops=10**8
    )
    blocks = call(
        functools.partial(
            filter_kernel, edges=False, taken=len(blocks), given=parts if pairwise[3] else 1
        ),
        sent(wide, pairwise[3]),
        (place, *blocks, sums, *filters),
        (slim_buffer, wide_buffer),
        flops=10**9,
    )
    blocks = exchange(blocks)
    (spread,) = call(spread_kernel, ((lax.axis_size("rows"), 1, lanes),), blocks)
    sums = lax.all_to_all(spread, "rows", split_axis=0, concat_axis=0, tiled=True)
    (second,) = call(
        second_kernel, (block,), (*blocks, image, tab["row_inverse"]), flops=10**8
    )
    return call(
        final_kernel,
        (block, block, block),
        (sums, search, grad, image, second),
        (pltpu.VMEM(block, jnp.float32),) * 3 + (pltpu.SemaphoreType.DMA((3, pieces)),),
        flops=10**6,
        far_out=True,
    )


def solution(mesh):
    placed = (P("rows", "cols"), P("rows", "cols"), P("rows", "cols"))
    return jax.shard_map(
        on_device,
        mesh=mesh,
        in_specs=placed,
        out_specs=placed,
        check_vma=False,
    )
```

```python
import functools
import math

import jax
import jax.numpy as jnp
import ml_dtypes
import numpy as np
from jax import lax
from jax.experimental import pallas as pl
from jax.experimental.pallas import tpu as pltpu
from jax.sharding import PartitionSpec as P

dispersion = 4.0
prior_scale = 0.25
kappa_sq = 0.05
weight_shift = 1.0
centre = kappa_sq + 4.0

band = 64
width = 2048
lanes = 128
tiles = width // lanes
parts = 8
total_cols = width * parts
lines = band // parts
half = 72
kept = 64
vmem_bytes = 48 * 1024 * 1024
pieces = 4


def high_low(table):
    high = table.astype(ml_dtypes.bfloat16)
    low = (table - high.astype(np.float64)).astype(ml_dtypes.bfloat16)
    return high, low


@functools.cache
def tables():
    rows = np.arange(band)
    freq = np.zeros(band)
    basis = np.zeros((band, band))
    basis[0] = 1.0 / math.sqrt(band)
    for k in range(1, band // 2):
        angle = 2.0 * np.pi * ((k * rows) % band) / band
        basis[2 * k - 1] = np.cos(angle) * math.sqrt(2.0 / band)
        basis[2 * k] = np.sin(angle) * math.sqrt(2.0 / band)
        freq[2 * k - 1] = freq[2 * k] = k
    basis[band - 1] = (1.0 - 2.0 * (rows % 2)) / math.sqrt(band)
    freq[band - 1] = band // 2
    row_term = kappa_sq + 4.0 * np.sin(np.pi * freq / band) ** 2
    out = {}
    high, low = high_low(basis)
    out["row_forward"] = np.concatenate([high, high, low], 1)
    share = np.zeros((band, 16))
    for row, at in ((0, 0), (1, 1), (2, band - 2), (3, band - 1)):
        share[:, row] = prior_scale * basis[:, at]
    share[:, 8 + 1] = prior_scale * basis[:, 0]
    share[:, 8 + 2] = prior_scale * basis[:, band - 1]
    high, low = high_low(share)
    out["halo_forward"] = np.concatenate([high, high, low], 1)
    high, low = high_low(basis.T)
    out["row_inverse"] = np.concatenate([high, high, low], 1)
    out["row_term"] = np.tile(row_term[:, None], (1, lanes)).astype(np.float32)

    count = lanes // 2 + 1
    outer = np.arange(count)
    inner = np.arange(lanes)
    angle = 2.0 * np.pi * ((outer[:, None] * inner[None, :]) % lanes) / lanes
    section = np.zeros((2 * half, lanes))
    section[:count] = np.cos(angle)
    section[half : half + count] = np.sin(angle)
    high, low = high_low(section)
    out["outer_forward"] = np.concatenate([high, high, low], 1)
    section = section.T.copy()
    section[:, half:] *= -1.0
    high, low = high_low(section)
    out["outer_inverse"] = np.concatenate([high, high, low], 1)

    angle = 2.0 * np.pi * outer[:, None] * inner[None, :] / total_cols
    twist = np.zeros((2, half, lanes), np.float32)
    twist[0, :count] = np.cos(angle)
    twist[1, :count] = np.sin(angle)
    out["twist"] = twist

    kept_inner = np.concatenate([np.arange(kept // 2), np.arange(lanes - kept // 2, lanes)])
    angle = 2.0 * np.pi * ((inner[:, None] * kept_inner[None, :]) % lanes) / lanes
    cosine, sine = np.cos(angle), np.sin(angle)
    high, low = high_low(np.block([[cosine, -sine], [sine, cosine]]))
    out["inner_forward"] = np.concatenate([high, low], 1)
    high, low = high_low(np.block([[cosine.T, sine.T], [-sine.T, cosine.T]]))
    out["inner_inverse"] = np.concatenate([high, high, low], 0)

    col_freq = outer[:, None] + lanes * kept_inner[None, :]
    quarter = total_cols // 4
    retained = (col_freq < quarter) | (col_freq > total_cols - quarter)
    twice = np.where((outer == 0) | (outer == lanes // 2), 1.0, 2.0)[:, None]
    weight = np.zeros((half, 2 * kept))
    weight[:count] = np.tile(np.where(retained, twice / total_cols, 0.0), (1, 2))
    term = np.zeros((half, 2 * kept))
    term[:count] = np.tile(4.0 * np.sin(np.pi * col_freq / total_cols) ** 2, (1, 2))
    out["weight"] = weight.astype(np.float32)
    out["col_term"] = term.astype(np.float32)
    return out


def split(value):
    high = value.astype(jnp.bfloat16)
    low = (value - high.astype(jnp.float32)).astype(jnp.bfloat16)
    return high, low


def dot(left, right):
    return jnp.dot(left, right, preferred_element_type=jnp.float32)


def left_product(table, value):
    high, low = split(value)
    return dot(table, jnp.concatenate([high, low, high], 0))


def lane_index(shape):
    return lax.broadcasted_iota(jnp.int32, shape, 1)


def neighbours(field):
    full = field.shape[1]
    return pltpu.roll(field, 1, 1) + pltpu.roll(field, full - 1, 1)


def stencil(pad):
    full = width + lanes
    field = pad[8:72, :]
    near = pad[7:71, :] + pad[9:73, :]
    far = pad[6:70, :] + pad[10:74, :]
    across = neighbours(2.0 * near - (2.0 * centre) * field)
    distant = far + pltpu.roll(field, 2, 1) + pltpu.roll(field, full - 2, 1)
    return prior_scale * ((centre * centre + 4.0) * field - 2.0 * centre * near + across + distant)


def halo_terms(place, swap_a, swap_b, halo):
    even = place[0] % 2 == 0
    span = swap_a.shape[1]
    halo[...] = jnp.zeros((8, width + lanes), jnp.float32)
    halo[0:2, :span] = jnp.where(even, swap_b[...], swap_a[...])
    halo[2:4, :span] = jnp.where(even, swap_a[...], swap_b[...])
    rows = halo[...]
    beside = 2.0 * neighbours(rows) - (2.0 * centre) * rows
    return rows, beside


def halo_rows(rows, beside):
    return prior_scale * jnp.concatenate(
        [
            beside[1:2] + rows[0:1],
            rows[1:2],
            jnp.zeros((4, width + lanes), jnp.float32),
            rows[2:3],
            beside[2:3] + rows[3:4],
        ],
        0,
    )


def add_halo_rows(field, added):
    index = lax.broadcasted_iota(jnp.int32, added.shape, 0)
    return jnp.concatenate(
        [
            field[:8] + jnp.where(index < 4, added, 0.0),
            field[8 : band - 8],
            field[band - 8 :] + jnp.where(index >= 4, added, 0.0),
        ],
        0,
    )


def store_coefs(place, coefs, buffer, outs, count):
    target = outs[0] if len(outs) == 1 else buffer
    for part in range(parts):
        for tile in range(count):
            target[part, tile * lines : (tile + 1) * lines, :] = coefs[
                part * lines : (part + 1) * lines, tile * lanes : (tile + 1) * lanes
            ]
    store_blocks(place, buffer, outs)


def store_blocks(place, buffer, outs):
    if len(outs) == 1:
        return
    for mask, out in enumerate(outs):
        out[...] = buffer[place[1] ^ mask]


def load_blocks(place, refs, buffer):
    if len(refs) == 1:
        return refs[0]
    for mask, ref in enumerate(refs):
        buffer[place[1] ^ mask] = ref[...]
    return buffer


def load_coefs(buffer, count):
    return jnp.concatenate(
        [
            jnp.concatenate(
                [buffer[part, tile * lines : (tile + 1) * lines, :] for part in range(parts)], 0
            )
            for tile in range(count)
        ],
        1,
    )


def gradient_kernel(
    latent, counts, exposure, basis, coefs, grad, fisher, pad, counts_here, exposure_here, sems
):
    fields = ((latent, pad), (exposure, exposure_here), (counts, counts_here))
    copies = []
    for which, (there, here) in enumerate(fields):
        skip = 8 if which == 0 else 0
        for part in range(pieces):
            rows = pl.ds(part * (band // pieces), band // pieces)
            onto = pl.ds(part * (band // pieces) + skip, band // pieces)
            copies.append(
                pltpu.make_async_copy(
                    there.at[rows, :], here.at[onto, :width], sems.at[which, part]
                )
            )
            copies[-1].start()
    pad[0:8, :] = jnp.zeros((8, width + lanes), jnp.float32)
    pad[72:80, :] = jnp.zeros((8, width + lanes), jnp.float32)
    pad[8:72, width:] = jnp.zeros((band, lanes), jnp.float32)
    for copy in copies[:pieces]:
        copy.wait()
    prior = stencil(pad)
    for copy in copies[pieces:]:
        copy.wait()
    mean_rate = exposure_here[...].astype(jnp.float32) * jnp.exp(pad[8:72, :width])
    ratio = dispersion / (dispersion + mean_rate)
    fisher[...] = mean_rate * ratio
    score = (counts_here[...].astype(jnp.float32) - mean_rate) * ratio
    inside = score - prior[:, :width]
    grad[...] = inside
    coefs[...] = left_product(basis[...], jnp.concatenate([inside, -prior[:, width:]], 1))


def gradient_halo_kernel(place, coefs, swap_a, swap_b, basis, *rest):
    *outs, added, halo, buffer = rest
    rows, beside = halo_terms(place, swap_a, swap_b, halo)
    added[...] = -halo_rows(rows, beside)
    whole = coefs[...] - left_product(basis[...], jnp.concatenate([rows, beside], 0))
    spill = whole[:, width:]
    spill = spill + pltpu.roll(spill, lanes // 2, 1)
    store_coefs(place, jnp.concatenate([whole[:, :width], spill], 1), buffer, outs, tiles + 1)


def gather_lines(incoming, edges):
    lane = lane_index((tiles, lanes))
    sub = lax.broadcasted_iota(jnp.int32, (tiles, lanes), 0)
    first = (sub == 0) & (lane < 2)
    last = (sub == tiles - 1) & (lane >= lanes - 2)
    line_fields = []
    for line in range(lines):
        blocks = [
            incoming[part, pl.ds(line, tiles, stride=lines), :] for part in range(parts)
        ]
        if edges:
            spill = [
                incoming[part, tiles * lines + line : tiles * lines + line + 1, :]
                for part in range(parts)
            ]
            for part in range(parts):
                if part > 0:
                    blocks[part] = blocks[part] + jnp.where(first, spill[part - 1], 0.0)
                if part < parts - 1:
                    blocks[part] = blocks[part] + jnp.where(last, spill[part + 1], 0.0)
        line_fields.append(jnp.concatenate(blocks, 0))
    return jnp.concatenate(line_fields, 1)


def columns_forward(field, outer_forward, inner_forward, twist):
    section = left_product(outer_forward[...], field)
    cosine, sine = twist[0], twist[1]
    turned = []
    for line in range(lines):
        cols = slice(line * lanes, (line + 1) * lanes)
        even_part, odd_part = section[:half, cols], section[half:, cols]
        real = even_part * cosine - odd_part * sine
        imag = -(odd_part * cosine + even_part * sine)
        turned.append(jnp.concatenate([real, imag], 1))
    high, low = split(jnp.concatenate(turned, 0))
    both = dot(high, inner_forward[...])
    return both[:, : 2 * kept] + both[:, 2 * kept :] + dot(low, inner_forward[:, : 2 * kept])


def scale_spectrum(place, spectrum, row_term, col_term, weight):
    row_line = row_term[pl.ds(pl.multiple_of(place[1] * lines, lines), lines), :]
    scaled = []
    total = jnp.zeros((half, 2 * kept), jnp.float32)
    for line in range(lines):
        inner_term = row_line[line : line + 1, :] + col_term[...]
        quad = prior_scale * inner_term * inner_term
        gain = -quad / (quad + weight_shift) * weight[...]
        piece = spectrum[line * half : (line + 1) * half, :]
        scaled.append(piece * gain)
        total = total + piece * scaled[-1]
    return jnp.concatenate(scaled, 0), total


def columns_inverse(scaled, outer_inverse, inner_inverse, twist):
    high, low = split(scaled)
    back = dot(jnp.concatenate([high, low], 1), inner_inverse[: 4 * kept, :]) + dot(
        high, inner_inverse[4 * kept :, :]
    )
    cosine, sine = twist[0], twist[1]
    reals, imags = [], []
    for line in range(lines):
        rows = slice(line * half, (line + 1) * half)
        real, imag = back[rows, :lanes], back[rows, lanes:]
        reals.append(real * cosine - imag * sine)
        imags.append(imag * cosine + real * sine)
    folded = jnp.concatenate([jnp.concatenate(reals, 1), jnp.concatenate(imags, 1)], 0)
    return left_product(outer_inverse[...], folded)


def store_lines(result, out):
    for line in range(lines):
        for part in range(parts):
            out[part, pl.ds(line, tiles, stride=lines), :] = result[
                part * tiles : (part + 1) * tiles, line * lanes : (line + 1) * lanes
            ]


def filter_kernel(place, *rest):
    blocks_in, rest = rest[:parts], rest[parts:]
    row_term, col_term, weight, outer_forward, inner_forward, twist, outer_inverse, inner_inverse = (
        rest[:8]
    )
    blocks_out, (incoming, out) = rest[8 : 8 + parts], rest[8 + parts :]
    incoming = load_blocks(place, blocks_in, incoming)
    field = gather_lines(incoming, True)
    spectrum = columns_forward(field, outer_forward, inner_forward, twist)
    scaled, _ = scale_spectrum(place, spectrum, row_term, col_term, weight)
    result = columns_inverse(scaled, outer_inverse, inner_inverse, twist)
    store_lines(result, out)
    edge_lane = lane_index((1, lanes))
    nothing = jnp.zeros((1, lanes), jnp.float32)
    for line in range(lines):
        cols = slice(line * lanes, (line + 1) * lanes)
        spot = tiles * lines + line
        for part in range(parts):
            after, before, from_left, from_right = nothing, nothing, nothing, nothing
            if part < parts - 1:
                row = slice((part + 1) * tiles, (part + 1) * tiles + 1)
                after = result[row, cols] + field[row, cols]
                from_right = incoming[part + 1, spot : spot + 1, :]
            if part > 0:
                row = slice(part * tiles - 1, part * tiles)
                before = result[row, cols] + field[row, cols]
                from_left = incoming[part - 1, spot : spot + 1, :]
            middle = jnp.where(edge_lane >= lanes // 2, from_left, from_right)
            out[part, spot : spot + 1, :] = jnp.where(
                edge_lane < 2, after, jnp.where(edge_lane >= lanes - 2, before, middle)
            )
    store_blocks(place, out, blocks_out)


def front_kernel(place, *rest):
    blocks_in, rest = rest[:parts], rest[parts:]
    sums, row_term, col_term, weight, outer_forward, inner_forward, twist = rest[:7]
    spectrum_out, known, incoming = rest[7:]
    incoming = load_blocks(place, blocks_in, incoming)
    field = gather_lines(incoming, False)
    spectrum = columns_forward(field, outer_forward, inner_forward, twist)
    scaled, total = scale_spectrum(place, spectrum, row_term, col_term, weight)
    spectrum_out[...] = scaled
    energy = jnp.sum(total, axis=(0, 1), keepdims=True)
    line = sums[...] + jnp.where(lane_index((1, lanes)) == 2, energy, 0.0)
    for part in range(parts):
        known[part] = line


def back_kernel(scaled, twist, outer_inverse, inner_inverse, out):
    store_lines(columns_inverse(scaled[...], outer_inverse, inner_inverse, twist), out)


def search_kernel(place, *rest):
    *blocks, grad, added, basis, full_grad, search, send_a, send_b, buffer = rest
    even = place[0] % 2 == 0
    buffer = load_blocks(place, blocks, buffer)
    update = left_product(basis[...], load_coefs(buffer, tiles + 1))
    beyond = update[:, width:]
    spill = pltpu.roll(beyond, lanes // 2, 1)
    lane = lane_index((band, lanes))
    base = add_halo_rows(grad[...], added[:, :width])
    head = base[:, :lanes] + jnp.where(lane < 2, spill, 0.0)
    tail = base[:, width - lanes :] + jnp.where(lane >= lanes - 2, spill, 0.0)
    whole = jnp.concatenate([head, base[:, lanes : width - lanes], tail], 1)
    full_grad[...] = whole
    found = jnp.concatenate([whole + update[:, :width], beyond], 1)
    search[...] = found
    top, bottom = found[:2, :], found[band - 2 :, :]
    send_a[...] = jnp.where(even, bottom, top)
    send_b[...] = jnp.where(even, top, bottom)


def image_kernel(search, fisher, basis, coefs, image, pad):
    pad[0:8, :] = jnp.zeros((8, width + lanes), jnp.float32)
    pad[72:80, :] = jnp.zeros((8, width + lanes), jnp.float32)
    pad[8:72, :] = search[...]
    result = stencil(pad)[:, :width] + fisher[...] * search[:, :width]
    image[...] = result
    coefs[...] = left_product(basis[...], result)


def image_halo_kernel(place, coefs, swap_a, swap_b, basis, *rest):
    *outs, added, halo, buffer = rest
    rows, beside = halo_terms(place, swap_a, swap_b, halo)
    added[...] = halo_rows(rows, beside)
    both = jnp.concatenate([rows, beside], 0)[:, :width]
    store_coefs(place, coefs[...] + left_product(basis[...], both), buffer, outs, tiles)


def sums_kernel(search, grad, partial, added, image, sums):
    field = search[:, :width]
    result = add_halo_rows(partial[...], added[:, :width])
    image[...] = result
    products = (grad[...] * field, field * result, result * result)
    lane = lane_index((1, lanes))
    line = jnp.zeros((1, lanes), jnp.float32)
    for which, product in enumerate(products):
        total = jnp.sum(product, axis=(0, 1), keepdims=True)
        line = line + jnp.where(lane == which, total, 0.0)
    sums[...] = line


def second_kernel(place, *rest):
    *blocks, image, basis, second, buffer = rest
    buffer = load_blocks(place, blocks, buffer)
    second[...] = image[...] + left_product(basis[...], load_coefs(buffer, tiles))


def final_kernel(
    sums, search, grad, image, second, step, residual, direction, step_here, residual_here, direction_here, sems
):
    total = jnp.sum(sums[...], axis=0)
    first_product = total[0:1, 0:1]
    curvature = total[0:1, 1:2]
    image_product = total[0:1, 2:3]
    step_size = first_product / curvature
    ratio = step_size * (image_product / curvature) - 1.0
    copies = []
    for part in range(pieces):
        rows = slice(part * (band // pieces), (part + 1) * (band // pieces))
        field = search[rows, :width]
        results = (
            (step_size * field, step_here, step),
            (grad[rows, :] - step_size * image[rows, :], residual_here, residual),
            ((field - step_size * second[rows, :]) + ratio * field, direction_here, direction),
        )
        for which, (value, here, there) in enumerate(results):
            here[rows, :] = value
            copies.append(
                pltpu.make_async_copy(here.at[rows, :], there.at[rows, :], sems.at[which, part])
            )
            copies[-1].start()
    for copy in copies:
        copy.wait()


def call(kernel, shapes, args, scratch=(), flops=0, far=0, far_out=False):
    in_specs = [
        pl.BlockSpec(memory_space=pltpu.HBM if i < far else pltpu.VMEM) for i in range(len(args))
    ]
    if args[0].ndim == 1:
        in_specs[0] = pl.BlockSpec(memory_space=pltpu.SMEM)
    outs = tuple(jax.ShapeDtypeStruct(s, jnp.float32) for s in shapes)
    moved = 4 * (sum(a.size for a in args) + sum(o.size for o in outs))
    return pl.pallas_call(
        kernel,
        out_shape=outs,
        in_specs=in_specs,
        out_specs=tuple(
            pl.BlockSpec(memory_space=pltpu.HBM if far_out else pltpu.VMEM) for _ in outs
        ),
        scratch_shapes=list(scratch),
        compiler_params=pltpu.CompilerParams(vmem_limit_bytes=vmem_bytes),
        cost_estimate=pl.CostEstimate(flops=flops, bytes_accessed=moved, transcendentals=0),
    )(*args)


def row_swaps():
    count = lax.axis_size("rows")
    inner = [(i, i ^ 1) for i in range(count)]
    outer = [(i, i + 1) for i in range(1, count - 1, 2)] + [(i + 1, i) for i in range(1, count - 1, 2)]
    return inner, outer


def exchange(blocks):
    if len(blocks) == 1:
        return [lax.all_to_all(blocks[0], "cols", split_axis=0, concat_axis=0, tiled=True)]
    count = lax.axis_size("cols")
    got = {}
    for mask in (1, 4, 2, 6, 3, 5, 7):
        got[mask] = lax.ppermute(blocks[mask], "cols", [(i, i ^ mask) for i in range(count)])
    return [blocks[0]] + [got[mask] for mask in range(1, parts)]


def swap_rows(send_a, send_b):
    inner, outer = row_swaps()
    return lax.ppermute(send_a, "rows", inner), lax.ppermute(send_b, "rows", outer)


def row_swap(value, mask):
    count = lax.axis_size("rows")
    return lax.ppermute(value, "rows", [(i, i ^ mask) for i in range(count)])


def on_device(latent, counts, exposure):
    consts = tables()
    tab = {name: jnp.asarray(value) for name, value in consts.items()}
    row_index = lax.axis_index("rows")
    place = jnp.stack([row_index, lax.axis_index("cols")]).astype(jnp.int32)
    full = width + lanes
    pad = pltpu.VMEM((80, full), jnp.float32)
    halo = pltpu.VMEM((8, full), jnp.float32)
    wide = ((tiles + 1) * lines, lanes)
    slim = (tiles * lines, lanes)
    wide_buffer = pltpu.VMEM((parts, *wide), jnp.float32)
    slim_buffer = pltpu.VMEM((parts, *slim), jnp.float32)
    block = (band, width)
    extended = (band, full)
    forward = [
        tab[name]
        for name in ("row_term", "col_term", "weight", "outer_forward", "inner_forward", "twist")
    ]
    inverse = [tab["outer_inverse"], tab["inner_inverse"]]

    even = row_index % 2 == 0
    top, bottom = latent[:2], latent[band - 2 :]
    swap_a, swap_b = swap_rows(jnp.where(even, bottom, top), jnp.where(even, top, bottom))
    coefs, grad_part, fisher = call(
        gradient_kernel,
        (extended, block, block),
        (
            *(pltpu.with_memory_space_constraint(a, pltpu.HBM) for a in (latent, counts, exposure)),
            tab["row_forward"],
        ),
        (
            pad,
            pltpu.VMEM(block, jnp.int32),
            pltpu.VMEM(block, jnp.int32),
            pltpu.SemaphoreType.DMA((3, pieces)),
        ),
        flops=10**9,
        far=3,
    )
    *blocks, added = call(
        gradient_halo_kernel,
        (wide,) * parts + ((8, full),),
        (place, coefs, swap_a, swap_b, tab["halo_forward"]),
        (halo, wide_buffer),
        flops=10**7,
    )
    blocks = exchange(blocks)
    blocks = call(
        filter_kernel,
        (wide,) * parts,
        (place, *blocks, *forward, *inverse),
        (wide_buffer, wide_buffer),
        flops=10**9,
    )
    blocks = exchange(blocks)
    grad, search, send_a, send_b = call(
        search_kernel,
        (block, extended, (2, full), (2, full)),
        (place, *blocks, grad_part, added, tab["row_inverse"]),
        (wide_buffer,),
        flops=10**8,
    )
    swap_a, swap_b = swap_rows(send_a, send_b)
    coefs, partial = call(
        image_kernel,
        (block, block),
        (search, fisher, tab["row_forward"]),
        (pad,),
        flops=10**9,
    )
    *blocks, added = call(
        image_halo_kernel,
        (slim,) * parts + ((8, full),),
        (place, coefs, swap_a, swap_b, tab["halo_forward"]),
        (halo, slim_buffer),
        flops=10**7,
    )
    blocks = exchange(blocks)
    image, sums = call(
        sums_kernel, (block, (1, lanes)), (search, grad, partial, added), flops=10**8
    )
    scaled, known = call(
        front_kernel,
        ((lines * half, 2 * kept), (parts, 1, lanes)),
        (place, *blocks, sums, *forward),
        (slim_buffer,),
        flops=10**8,
    )
    (block_out,) = call(
        back_kernel, ((parts, *slim),), (scaled, tab["twist"], *inverse), flops=10**9
    )
    block_out, known = lax.optimization_barrier((block_out, known + row_swap(known, 1)))
    blocks = exchange([block_out])
    known = known + row_swap(known, 2) + row_swap(known, 4) + row_swap(known, 6)
    known = known + row_swap(known, 8) + row_swap(known, 16) + row_swap(known, 24)
    sums = exchange([known])[0]
    (second,) = call(
        second_kernel,
        (block,),
        (place, *blocks, image, tab["row_inverse"]),
        (slim_buffer,),
        flops=10**8,
    )
    return call(
        final_kernel,
        (block, block, block),
        (sums, search, grad, image, second),
        (pltpu.VMEM(block, jnp.float32),) * 3 + (pltpu.SemaphoreType.DMA((3, pieces)),),
        flops=10**6,
        far_out=True,
    )


def solution(mesh):
    placed = (P("rows", "cols"), P("rows", "cols"), P("rows", "cols"))
    return jax.shard_map(
        on_device,
        mesh=mesh,
        in_specs=placed,
        out_specs=placed,
        check_vma=False,
    )
```
